512 devices in a mesh: dp: 32 (over x, z_lo), tensor: 16 (over y, z_hi, core).
Axes of the slice: x: 4, y: 4, z: 16 (z_hi: 2, z_lo: 8; z = z_hi * 8 + z_lo), core: 2. Of those that a mesh axis runs over, the one named last changes fastest.
Arguments:
- owner_states: float32 [64, 32, 128, 128], P('dp', 'tensor'), may hold values from -6 to 6
- sample_slot: int32 [1024], P('dp'), may hold values from 0 to 1023, each once
- query_in: bfloat16 [1024, 4, 2048], P('dp', None, 'tensor'), may hold values from -6 to 6
- key_in: bfloat16 [1024, 4, 2048], P('dp', None, 'tensor'), may hold values from -6 to 6
- value_in: bfloat16 [1024, 4, 4096], P('dp', None, 'tensor'), may hold values from -6 to 6
- gate_in: bfloat16 [1024, 4, 4096], P('dp', None, 'tensor'), may hold values from -6 to 6
- decay_in: float32 [1024, 4, 2, 32], P('dp', None, None, 'tensor'), may hold values from -6 to 6
- decay_rate: float32 [32], P('tensor'), may hold values from 0.05 to 2
- dt_bias: float32 [32], P('tensor'), may hold values from -4 to 4
- norm_gain: float32 [128], replicated, may hold values from 0.25 to 1.75
- out_weight: bfloat16 [4096, 2048], P('tensor'), may hold values from -0.09375 to 0.09375
Outputs:
- mixed: bfloat16 [1024, 4, 2048], P('dp', None, 'tensor')
- final_states: bfloat16 [1024, 32, 128, 128], P('dp', 'tensor')
The draws below stay inside these ranges and needn't reach their ends.
Inputs may be any that keep to these rules, and one draw needn't show every extreme that they name: `sample_slot`: each slot appears once, so each prompt has exactly 16 rows, placed anywhere.
All inputs are finite; a program needn't handle non-finite values.
Results may differ from the reference program's by a relative error of at most 0.0049.
Values sent between devices are 32-bit elements; how exact they have to be, the bound alone decides.
A program may use at most 64 MiB of HBM per device.

```python
import math
import jax
import jax.numpy as jnp
from jax import lax

D = 2048
HV = 32
HK = 16
DK = 128
DV = 128
SAMPLES = 16
STEPS = 4
PROMPTS = 64
ROWS = 1024


def shard_levels(own_key, shape, shards, least, high):
    level, own = 1.0, jax.random.fold_in(own_key, 6)
    for position, parts in shards:
        heights = jnp.exp(jax.random.uniform(jax.random.fold_in(own, position), (parts,), jnp.float32, least / len(shards), high / len(shards)))
        level = level * jnp.repeat(heights, shape[position] // parts).reshape([-1 if axis == position else 1 for axis in range(len(shape))])
    return level


def bell_draw(own_key, shape, scale, limit, split=(), kind=jnp.bfloat16):
    values = jax.random.normal(own_key, shape, jnp.float32) * scale
    if len(split) > 0:
        values = shard_levels(own_key, shape, split, -0.22, 0.18) * values
    return jnp.clip(values, min=-limit, max=limit).astype(kind)


def setup_inputs(seed: int = 0) -> dict:
    key_list = jax.random.split(jax.random.key(seed), 12)
    owner_states = bell_draw(key_list[0], (PROMPTS, HV, DV, DK), 1.0, 6.0, ((0, 32), (1, 16)), jnp.float32)
    sample_slot = jax.random.permutation(key_list[1], ROWS).astype(jnp.int32)
    query_in = bell_draw(key_list[2], (ROWS, STEPS, HK * DK), 1.0, 6.0, ((0, 32), (2, 16)))
    key_in = bell_draw(key_list[3], (ROWS, STEPS, HK * DK), 1.0, 6.0, ((0, 32), (2, 16)))
    value_in = bell_draw(key_list[4], (ROWS, STEPS, HV * DV), 1.0, 6.0, ((0, 32), (2, 16)))
    gate_in = bell_draw(key_list[5], (ROWS, STEPS, HV * DV), 1.0, 6.0, ((0, 32), (2, 16)))
    decay_in = bell_draw(key_list[6], (ROWS, STEPS, 2, HV), 1.5, 6.0, ((0, 32), (3, 16)), jnp.float32)
    decay_rate = jnp.clip(jnp.exp(math.log(2.0) - 3.6888794 * jax.random.uniform(key_list[7], (HV,), jnp.float32) ** shard_levels(key_list[7], (HV,), ((0, 16),), -0.2, 0.2)), 0.05, 2.0)
    dt_bias = bell_draw(key_list[8], (HV,), 1.0, 4.0, ((0, 16),), jnp.float32)
    norm_gain = jnp.clip(1.0 + 0.15 * jax.random.normal(key_list[9], (DV,), jnp.float32), 0.25, 1.75)
    out_weight = bell_draw(key_list[10], (HV * DV, D), (HV * DV) ** -0.5, 0.09375, ((0, 16),))
    return dict(owner_states=owner_states, sample_slot=sample_slot, query_in=query_in, key_in=key_in, value_in=value_in, gate_in=gate_in, decay_in=decay_in, decay_rate=decay_rate, dt_bias=dt_bias, norm_gain=norm_gain, out_weight=out_weight)


def unit_rows(values):
    return values / jnp.sqrt(lax.optimization_barrier(jnp.sum(values * values, axis=-1, keepdims=True)) + 1e-06)

def decode_block(start, query_in, key_in, value_in, gate_in, decay_in, decay_rate, dt_bias, norm_gain, out_weight):
    rows = query_in.shape[0]
    steps = query_in.shape[1]
    queries = unit_rows(query_in.astype(jnp.float32).reshape(rows, steps, -1, DK)) / jnp.sqrt(jnp.float32(DK))
    keys_all = unit_rows(key_in.astype(jnp.float32).reshape(rows, steps, -1, DK))
    queries = jnp.repeat(queries, 2, axis=2)
    keys_all = jnp.repeat(keys_all, 2, axis=2)
    values = value_in.astype(jnp.float32).reshape(rows, steps, -1, DV)
    gates = gate_in.astype(jnp.float32).reshape(rows, steps, -1, DV)
    beta = jax.nn.sigmoid(decay_in[:, :, 1])
    alpha = jnp.exp(-decay_rate * jax.nn.softplus(decay_in[:, :, 0] + dt_bias))
    state = start
    outputs = []
    for step in range(steps):
        state = alpha[:, step, :, None, None] * state
        recalled = jnp.einsum('bhvk,bhk->bhv', state, keys_all[:, step], precision=lax.Precision.HIGHEST)
        error = values[:, step] - recalled
        state = state + beta[:, step, :, None, None] * error[:, :, :, None] * keys_all[:, step, :, None, :]
        outputs.append(jnp.einsum('bhvk,bhk->bhv', state, queries[:, step], precision=lax.Precision.HIGHEST))
    output = jnp.stack(outputs, axis=1)
    scale = lax.rsqrt(lax.optimization_barrier(jnp.mean(output * output, axis=-1, keepdims=True)) + 1e-06)
    hidden = (output * scale * norm_gain * jax.nn.silu(gates)).astype(jnp.bfloat16).reshape(rows, steps, -1)
    mixed = jnp.einsum('rsc,cd->rsd', hidden.astype(jnp.float32), out_weight.astype(jnp.float32), precision=lax.Precision.HIGHEST)
    return (mixed.astype(jnp.bfloat16), state.astype(jnp.bfloat16))

def reference(owner_states, sample_slot, query_in, key_in, value_in, gate_in, decay_in, decay_rate, dt_bias, norm_gain, out_weight):
    blocks = ROWS // SAMPLES
    prompt = (sample_slot // SAMPLES).astype(jnp.int32)

    def one_block(items):
        block_prompt, block_query, block_key, block_value, block_gate, block_decay = items
        start = jnp.take(owner_states, block_prompt, axis=0)
        return decode_block(start, block_query, block_key, block_value, block_gate, block_decay, decay_rate, dt_bias, norm_gain, out_weight)
    items = (prompt.reshape(blocks, SAMPLES), query_in.reshape(blocks, SAMPLES, STEPS, -1), key_in.reshape(blocks, SAMPLES, STEPS, -1), value_in.reshape(blocks, SAMPLES, STEPS, -1), gate_in.reshape(blocks, SAMPLES, STEPS, -1), decay_in.reshape(blocks, SAMPLES, STEPS, 2, HV))
    mixed, final_states = lax.map(one_block, items)
    return (mixed.reshape(ROWS, STEPS, D), final_states.reshape(ROWS, HV, DV, DK))
```

```python
import functools

import jax
import jax.numpy as jnp
from jax import lax
from jax.experimental import pallas as pl
from jax.experimental.pallas import tpu as pltpu
from jax.sharding import PartitionSpec as P

MESH = pl.DeviceIdType.MESH
F32 = jnp.float32
BF16 = jnp.bfloat16
NX, NZ = 4, 8
ROWS, STEPS, DK, DV, HEADS = 32, 4, 128, 128, 2
SAMPLES = 16
TAIL = 32
HEAD = HEADS * DV - TAIL
LAG_X = 3
LAG_T = 3
CHUNKS = 2
CROWS = ROWS * STEPS // CHUNKS
PAIRS = [(s, t) for t in range(STEPS) for s in range(t + 1)]


def split(value):
    high = value.astype(BF16).astype(F32)
    return high, value - high


def kernel(
    own, slot, kq_in, v_in, gate_in, decay_in, rate, bias, gain, weight,
    mixed, final,
    g, kq, kq2, kl, ca, cb, cc, cd, ce, gs, gk, wl, hid, fs,
    part, mine, got1, got2, got3, acc,
    zr, xrp, xrm, xo, zsr, zsl, xsp, xsm, fsp, fsm,
    ar, asd, azr, azsr, azsl, s1, r1, s2, r2, s3, r3, fsem, lsem,
):
    dp = lax.axis_index("dp")
    tn = lax.axis_index("tensor")
    x = dp // NZ
    z = dp % NZ
    xp = (x + 1) % NX
    xm = (x + 3) % NX
    y = tn // 4
    zh = (tn // 2) % 2
    core = tn % 2

    def tensor_of(yy, zz, cc_):
        return (yy * 2 + zz) * 2 + cc_

    def rc(src, dst, ss, rs, xx, zz):
        return pltpu.make_async_remote_copy(
            src_ref=src, dst_ref=dst, send_sem=ss, recv_sem=rs,
            device_id=(xx * NZ + zz, tn), device_id_type=MESH,
        )

    def tc(src, dst, ss, rs, to):
        return pltpu.make_async_remote_copy(
            src_ref=src, dst_ref=dst, send_sem=ss, recv_sem=rs,
            device_id=(dp, to), device_id_type=MESH,
        )

    local = pltpu.make_async_copy(own, g.at[x, z], lsem)
    local.start()

    bar = pltpu.get_barrier_semaphore()

    def sig(d, t):
        pl.semaphore_signal(bar, inc=1, device_id=(d, t), device_id_type=MESH)

    partner = tensor_of(y, zh, 1 - core)
    far = tensor_of(y, 1 - zh, core)
    sig(dp, far)
    sig(dp, tensor_of((y + 2) % 4, zh, core))
    sig(dp, tensor_of((y + 1) % 4, zh, core))
    sig(dp, tensor_of((y + 3) % 4, zh, core))
    sig(xp * NZ + z, tn)
    sig(xm * NZ + z, tn)

    @pl.when(z > 0)
    def _():
        sig(dp - 1, tn)

    @pl.when(z < NZ - 1)
    def _():
        sig(dp + 1, tn)

    sig(dp, partner)
    edge = jnp.logical_or(z == 0, z == NZ - 1)

    @pl.when(edge)
    def _():
        pl.semaphore_wait(bar, 8)

    @pl.when(jnp.logical_not(edge))
    def _():
        pl.semaphore_wait(bar, 9)

    def blk(xx, zp, h):
        return g.at[xx, zp, h, pl.ds(0, HEAD)]

    def z_right(zp, h, src):
        return rc(src, blk(x, zp, h), zsr.at[zp, h], zr.at[zp, h], x, z + 1)

    def z_left(zp, h, src):
        return rc(src, blk(x, zp, h), zsl.at[zp, h], zr.at[zp, h], x, z - 1)

    def x_plus(zp, h, src):
        return rc(src, blk(x, zp, h), xsp.at[zp, h], xrp.at[zp, h], xp, z)

    def x_minus(zp, h, src):
        return rc(src, blk(x, zp, h), xsm.at[zp, h], xrm.at[zp, h], xm, z)

    def f_plus(zp):
        return rc(blk(xm, zp, 0), blk(xm, zp, 0), fsp.at[zp], xo.at[zp, 0], xp, z)

    def f_minus(zp):
        return rc(blk(xp, zp, 1), blk(xp, zp, 1), fsm.at[zp], xo.at[zp, 1], xm, z)

    def tail(xx):
        return g.at[xx, z, :, pl.ds(HEAD, TAIL)]

    def tail_half(xx, h):
        return g.at[xx, z, h, pl.ds(HEAD, TAIL)]

    def t_plus(src):
        return rc(src, tail(x), asd.at[0], ar.at[0], xp, z)

    def t_minus(src):
        return rc(src, tail(x), asd.at[1], ar.at[1], xm, z)

    def tf_plus():
        return rc(tail_half(xm, 0), tail_half(xm, 0), asd.at[2], ar.at[2], xp, z)

    def tf_minus():
        return rc(tail_half(xp, 1), tail_half(xp, 1), asd.at[3], ar.at[3], xm, z)

    def tails(zp):
        return g.at[:, zp, :, pl.ds(HEAD, TAIL)]

    def tz_right(zp):
        return rc(tails(zp), tails(zp), azsr.at[zp], azr.at[zp], x, z + 1)

    def tz_left(zp):
        return rc(tails(zp), tails(zp), azsl.at[zp], azr.at[zp], x, z - 1)

    t_plus(own.at[:, pl.ds(HEAD, TAIL)]).start()
    t_minus(own.at[:, pl.ds(HEAD, TAIL)]).start()
    for h in range(2):
        src = own.at[h, pl.ds(0, HEAD)]

        @pl.when(z < NZ - 1)
        def _():
            z_right(z, h, src).start()

        @pl.when(z > 0)
        def _():
            z_left(z, h, src).start()

        x_plus(z, h, src).start()
        x_minus(z, h, src).start()
    rc(tail(xm), tail(xm), asd.at[0], ar.at[0], xp, z).wait_recv()
    tf_plus().start()
    rc(tail(xp), tail(xp), asd.at[1], ar.at[1], xm, z).wait_recv()
    tf_minus().start()

    def prepare_keys():
        raw = kq_in[...].astype(F32)
        unit = raw * lax.rsqrt(jnp.sum(raw * raw, axis=1, keepdims=True) + 1e-6)
        kind = lax.broadcasted_iota(jnp.int32, unit.shape, 0) % 8
        unit = jnp.where(kind >= STEPS, unit * (DK**-0.5), unit)
        kq[...] = unit
        high, low = split(unit)
        for i in range(2 * STEPS):
            one = kq[pl.ds(i, ROWS, stride=8), :]
            high, low = split(one)
            kq2[pl.ds(i, ROWS, stride=16), :] = high
            kq2[pl.ds(i + 8, ROWS, stride=16), :] = low
            if i < STEPS:
                kl[pl.ds(i, ROWS, stride=16), :] = high
                kl[pl.ds(i + 4, ROWS, stride=16), :] = high
                kl[pl.ds(i + 8, ROWS, stride=16), :] = low
                kl[pl.ds(i + 12, ROWS, stride=16), :] = jnp.zeros_like(low)

    def prepare_gates():
        shape = (ROWS, DV)
        keys = [kq[pl.ds(i, ROWS, stride=8), :] for i in range(2 * STEPS)]
        kk, kqd = {}, {}
        for s, t in PAIRS:
            if s < t:
                kk[s, t] = jnp.sum(keys[s] * keys[t], axis=1, keepdims=True)
            kqd[s, t] = jnp.sum(keys[s] * keys[STEPS + t], axis=1, keepdims=True)
        for h in range(HEADS):
            alpha = []
            for t in range(STEPS):
                d = decay_in[:, pl.ds(t * 4 + h, 1)] + bias[h]
                soft = jnp.maximum(d, 0.0) + jnp.log1p(jnp.exp(-jnp.abs(d)))
                alpha.append(jnp.exp(-rate[h] * soft))
                b = decay_in[:, pl.ds(t * 4 + 2 + h, 1)]
                cb[h, t] = jnp.broadcast_to(1.0 / (1.0 + jnp.exp(-b)), shape)
            for t in range(STEPS):
                run = None
                for s in range(t, -1, -1):
                    n = PAIRS.index((s, t))
                    dot = kqd[s, t]
                    cd[h, n] = jnp.broadcast_to(dot if run is None else run * dot, shape)
                    if s < t:
                        cc[h, n] = jnp.broadcast_to(run * kk[s, t], shape)
                    if t == STEPS - 1:
                        ce[h, s] = jnp.broadcast_to(
                            jnp.ones_like(dot) if run is None else run, shape
                        )
                    run = alpha[s] if run is None else run * alpha[s]
                ca[h, t] = jnp.broadcast_to(run, shape)
                gate = gate_in[:, pl.ds((t * HEADS + h) * DV, DV)].astype(F32)
                gs[h, t] = gain[...] * gate / (1.0 + jnp.exp(-gate))

    def forward(zp):
        rc(blk(xm, zp, 0), blk(xm, zp, 0), fsp.at[zp], xrp.at[zp, 0], xp, z).wait_recv()
        f_plus(zp).start()
        rc(blk(xp, zp, 1), blk(xp, zp, 1), fsm.at[zp], xrm.at[zp, 1], xm, z).wait_recv()
        f_minus(zp).start()

    def gather_step(s, carry):
        zl = z - s
        zg = z + s
        for h in range(2):

            @pl.when(jnp.logical_and(s < NZ, zl >= 0))
            def _():
                z_right(zl, h, blk(x, zl, h)).wait_recv()

                @pl.when(z < NZ - 1)
                def _():
                    z_right(zl, h, blk(x, zl, h)).start()

                x_plus(zl, h, blk(x, zl, h)).start()
                x_minus(zl, h, blk(x, zl, h)).start()

            @pl.when(jnp.logical_and(s < NZ, zg < NZ))
            def _():
                z_left(zg, h, blk(x, zg, h)).wait_recv()

                @pl.when(z > 0)
                def _():
                    z_left(zg, h, blk(x, zg, h)).start()

                x_plus(zg, h, blk(x, zg, h)).start()
                x_minus(zg, h, blk(x, zg, h)).start()

        d = s - LAG_T

        @pl.when(d == 0)
        def _():
            rc(tail_half(x, 0), tail_half(x, 0), asd.at[2], ar.at[2], xp, z).wait_recv()
            rc(tail_half(x, 1), tail_half(x, 1), asd.at[3], ar.at[3], xm, z).wait_recv()
            local.wait()

            @pl.when(z < NZ - 1)
            def _():
                tz_right(z).start()

            @pl.when(z > 0)
            def _():
                tz_left(z).start()

        @pl.when(jnp.logical_and(d >= 1, z - d >= 0))
        def _():
            tz_right(z - d).wait_recv()

            @pl.when(z < NZ - 1)
            def _():
                tz_right(z - d).start()

        @pl.when(jnp.logical_and(d >= 1, z + d < NZ))
        def _():
            tz_left(z + d).wait_recv()

            @pl.when(z > 0)
            def _():
                tz_left(z + d).start()

        e = s - LAG_X

        @pl.when(jnp.logical_and(e >= 0, z - e >= 0))
        def _():
            forward(z - e)

        @pl.when(jnp.logical_and(e >= 1, z + e < NZ))
        def _():
            forward(z + e)

        @pl.when(s == 1)
        def _():
            prepare_keys()

        @pl.when(s == 2)
        def _():
            prepare_gates()

        return carry

    lax.fori_loop(1, NZ + max(LAG_X, LAG_T), gather_step, 0)

    def last_blocks(zp, carry):
        rc(blk(xm, zp, 1), blk(xm, zp, 1), xsp.at[zp, 1], xrp.at[zp, 1], xp, z).wait_recv()
        rc(blk(xp, zp, 0), blk(xp, zp, 0), xsm.at[zp, 0], xrm.at[zp, 0], xm, z).wait_recv()
        f_plus(zp).wait_recv()
        f_minus(zp).wait_recv()
        return carry

    lax.fori_loop(0, NZ, last_blocks, 0)

    contract = (((1,), (1,)), ((), ()))

    def state_of(r):
        p = slot[r] // SAMPLES
        return g[p // (2 * NZ), (p // 2) % NZ, p % 2]

    def recall(r, carry):
        high, low = split(state_of(r))
        both = kq2[pl.ds(pl.multiple_of(r * 16, 16), 16), :].astype(BF16)
        a = lax.dot_general(both, high.astype(BF16), contract, preferred_element_type=F32)
        b = lax.dot_general(both, low.astype(BF16), contract, preferred_element_type=F32)
        total = a[0:8] + a[8:16] + b[0:8]
        at = pl.ds(pl.multiple_of(r * 8, 8), 8)
        gk[0, at, :] = total[:, 0:DV]
        gk[1, at, :] = total[:, DV:]
        return carry

    lax.fori_loop(0, ROWS, recall, 0, unroll=4)

    for h in range(HEADS):
        u = []
        for t in range(STEPS):
            seen = ca[h, t] * gk[h, pl.ds(t, ROWS, stride=8), :]
            out = ca[h, t] * gk[h, pl.ds(STEPS + t, ROWS, stride=8), :]
            for s in range(t):
                seen = seen + cc[h, PAIRS.index((s, t))] * u[s]
            value = v_in[:, pl.ds((t * HEADS + h) * DV, DV)].astype(F32)
            u.append(cb[h, t] * (value - seen))
            for s in range(t + 1):
                out = out + cd[h, PAIRS.index((s, t))] * u[s]
            scale = lax.rsqrt(jnp.mean(out * out, axis=1, keepdims=True) + 1e-6)
            hid[pl.ds(t * ROWS, ROWS), pl.ds(h * DV, DV)] = (out * scale * gs[h, t]).astype(BF16)
        for s in range(STEPS):
            high, low = split(ce[h, s] * u[s])
            wl[h, pl.ds(s, ROWS, stride=16), :] = high
            wl[h, pl.ds(s + 4, ROWS, stride=16), :] = low
            wl[h, pl.ds(s + 8, ROWS, stride=16), :] = high
            wl[h, pl.ds(s + 12, ROWS, stride=16), :] = jnp.zeros_like(high)

    def product(c, yy, zz, cr):
        at = tensor_of(yy, zz, cr) * 128
        return jnp.dot(
            hid[pl.ds(c * CROWS, CROWS), :],
            weight[:, pl.ds(pl.multiple_of(at, 128), 128)],
            preferred_element_type=F32,
        )

    def cross(c, yy):
        return tc(part.at[c, yy], got1.at[c, yy], s1.at[c, yy], r1.at[c, yy], partner)

    def along_y(c, hop):
        yy = (y + hop) % 4
        return tc(
            mine.at[c, yy], got2.at[c, hop - 1], s2.at[c, hop - 1], r2.at[c, hop - 1],
            tensor_of(yy, zh, core),
        )

    def along_z(c):
        return tc(acc.at[c, 1 - zh], got3.at[c], s3.at[c], r3.at[c], far)

    hops = (2, 1, 3, 0)
    for c in range(CHUNKS):
        for hop in hops:
            yy = (y + hop) % 4
            for zz in range(2):
                part[c, yy, zz] = product(c, yy, zz, 1 - core)
            cross(c, yy).start()
    for c in range(CHUNKS):
        for hop in hops:
            yy = (y + hop) % 4
            for zz in range(2):
                mine[c, yy, zz] = product(c, yy, zz, core)
            cross(c, yy).wait_recv()
            mine[c, yy] = mine[c, yy] + got1[c, yy]
            if hop:
                along_y(c, hop).start()

    def finish(r, carry):
        state = state_of(r)
        at = pl.ds(pl.multiple_of(r * 16, 16), 16)
        keys = kl[at, :].astype(BF16)
        for h in range(HEADS):
            update = lax.dot_general(
                wl[h, at, :].astype(BF16), keys, (((0,), (0,)), ((), ())),
                preferred_element_type=F32,
            )
            decay = ca[h, STEPS - 1, pl.ds(r, 1), :]
            fs[r, pl.ds(h * DV, DV), :] = (
                decay * state[h * DV : (h + 1) * DV] + update
            ).astype(BF16)
        return carry

    def write(i):
        part_rows = pl.ds(i * (ROWS // 2), ROWS // 2)
        return pltpu.make_async_copy(fs.at[part_rows], final.at[part_rows], fsem.at[i])

    lax.fori_loop(0, ROWS // 2, finish, 0, unroll=2)
    write(0).start()
    for c in range(CHUNKS):
        for hop in (1, 3, 2):
            along_y(c, hop).wait_recv()
        acc[c] = mine[c, y] + got2[c, 0] + got2[c, 1] + got2[c, 2]
        along_z(c).start()
    lax.fori_loop(ROWS // 2, ROWS, finish, 0, unroll=2)
    write(1).start()
    for c in range(CHUNKS):
        along_z(c).wait_recv()
        done = (acc[c, zh] + got3[c]).astype(BF16)
        for i in range(STEPS // CHUNKS):
            t = c * (STEPS // CHUNKS) + i
            mixed[:, pl.ds(t * 128, 128)] = done[i * ROWS : (i + 1) * ROWS]

    t_plus(tail(x)).wait_send()
    t_minus(tail(x)).wait_send()
    tf_plus().wait_send()
    tf_minus().wait_send()

    def sent(zp, carry):
        for h in range(2):
            x_plus(zp, h, blk(x, zp, h)).wait_send()
            x_minus(zp, h, blk(x, zp, h)).wait_send()

            @pl.when(jnp.logical_and(z < NZ - 1, zp <= z))
            def _():
                z_right(zp, h, blk(x, zp, h)).wait_send()

            @pl.when(jnp.logical_and(z > 0, zp >= z))
            def _():
                z_left(zp, h, blk(x, zp, h)).wait_send()

        @pl.when(jnp.logical_and(z < NZ - 1, zp <= z))
        def _():
            tz_right(zp).wait_send()

        @pl.when(jnp.logical_and(z > 0, zp >= z))
        def _():
            tz_left(zp).wait_send()

        f_plus(zp).wait_send()
        f_minus(zp).wait_send()
        return carry

    lax.fori_loop(0, NZ, sent, 0)
    for c in range(CHUNKS):
        for yy in range(4):
            cross(c, yy).wait_send()
        for hop in (1, 2, 3):
            along_y(c, hop).wait_send()
        along_z(c).wait_send()
    write(0).wait()
    write(1).wait()


def body(
    owner_states, sample_slot, query_in, key_in, value_in, gate_in, decay_in,
    decay_rate, dt_bias, norm_gain, out_weight,
):
    kq = jnp.concatenate([key_in, query_in], axis=1).reshape(ROWS * 8, DK)
    vmem = pl.BlockSpec(memory_space=pltpu.VMEM)
    smem = pl.BlockSpec(memory_space=pltpu.SMEM)
    anywhere = pl.BlockSpec(memory_space=pl.ANY)
    dma = pltpu.SemaphoreType.DMA
    npair = len(PAIRS)
    mixed, final = pl.pallas_call(
        kernel,
        out_shape=(
            jax.ShapeDtypeStruct((ROWS, STEPS * 128), BF16),
            jax.ShapeDtypeStruct((ROWS, HEADS * DV, DK), BF16),
        ),
        in_specs=[anywhere, smem, vmem, vmem, vmem, vmem, smem, smem, vmem, vmem],
        out_specs=(vmem, anywhere),
        scratch_shapes=[
            pltpu.VMEM((NX, NZ, 2, HEADS * DV, DK), F32),
            pltpu.VMEM((ROWS * 8, DK), F32),
            pltpu.VMEM((ROWS * 16, DK), F32),
            pltpu.VMEM((ROWS * 16, DK), F32),
            pltpu.VMEM((HEADS, STEPS, ROWS, DV), F32),
            pltpu.VMEM((HEADS, STEPS, ROWS, DV), F32),
            pltpu.VMEM((HEADS, npair, ROWS, DV), F32),
            pltpu.VMEM((HEADS, npair, ROWS, DV), F32),
            pltpu.VMEM((HEADS, STEPS, ROWS, DV), F32),
            pltpu.VMEM((HEADS, STEPS, ROWS, DV), F32),
            pltpu.VMEM((HEADS, ROWS * 8, DV), F32),
            pltpu.VMEM((HEADS, ROWS * 16, DV), F32),
            pltpu.VMEM((ROWS * STEPS, HEADS * DV), BF16),
            pltpu.VMEM((ROWS, HEADS * DV, DK), BF16),
            pltpu.VMEM((CHUNKS, 4, 2, CROWS, 128), F32),
            pltpu.VMEM((CHUNKS, 4, 2, CROWS, 128), F32),
            pltpu.VMEM((CHUNKS, 4, 2, CROWS, 128), F32),
            pltpu.VMEM((CHUNKS, 3, 2, CROWS, 128), F32),
            pltpu.VMEM((CHUNKS, CROWS, 128), F32),
            pltpu.VMEM((CHUNKS, 2, CROWS, 128), F32),
        ]
        + [dma((NZ, 2)) for _ in range(8)]
        + [dma((NZ,)), dma((NZ,)), dma((4,)), dma((4,)), dma((NZ,)), dma((NZ,)), dma((NZ,))]
        + [dma((CHUNKS, 4)), dma((CHUNKS, 4)), dma((CHUNKS, 3)), dma((CHUNKS, 3))]
        + [dma((CHUNKS,)), dma((CHUNKS,)), dma((2,)), dma],
        compiler_params=pltpu.CompilerParams(
            collective_id=0, has_side_effects=True, vmem_limit_bytes=40 * 2**20
        ),
    )(
        owner_states.reshape(2, HEADS * DV, DK),
        sample_slot,
        kq,
        value_in.reshape(ROWS, STEPS * HEADS * DV),
        gate_in.reshape(ROWS, STEPS * HEADS * DV),
        decay_in.reshape(ROWS, STEPS * 2 * HEADS),
        decay_rate,
        dt_bias,
        norm_gain.reshape(1, DV),
        out_weight,
    )
    return mixed.reshape(ROWS, STEPS, 128), final.reshape(ROWS, HEADS, DV, DK)


def solution(mesh):
    return jax.shard_map(
        body,
        mesh=mesh,
        in_specs=(
            P("dp", "tensor", None, None),
            P("dp"),
            P("dp", None, "tensor"),
            P("dp", None, "tensor"),
            P("dp", None, "tensor"),
            P("dp", None, "tensor"),
            P("dp", None, None, "tensor"),
            P("tensor"),
            P("tensor"),
            P(),
            P("tensor", None),
        ),
        out_specs=(P("dp", None, "tensor"), P("dp", "tensor", None, None)),
        check_vma=False,
    )
```

```python
import functools

import jax
import jax.numpy as jnp
from jax import lax
from jax.experimental import pallas as pl
from jax.experimental.pallas import tpu as pltpu
from jax.sharding import PartitionSpec as P

MESH = pl.DeviceIdType.MESH
F32 = jnp.float32
BF16 = jnp.bfloat16
NX, NZ = 4, 8
ROWS, STEPS, DK, DV, HEADS = 32, 4, 128, 128, 2
SAMPLES = 16
TAIL = 40
HEAD = HEADS * DV - TAIL
FIRST, APART = 14, 3
LAG_T = 3
CHUNKS = 2
PIECES = 8
CROWS = ROWS * STEPS // CHUNKS
PAIRS = [(s, t) for t in range(STEPS) for s in range(t + 1)]


def split(value):
    high = value.astype(BF16).astype(F32)
    return high, value - high


def kernel(
    own, slot_in, q_in, k_in, v_in, gate_in, decay_in, rate_in, bias_in, gain_in, weight_in,
    mixed, final,
    slot, qb, kb, vb, gb, db, rate, bias, gain, weight,
    g, q32, k32, v32, g32, dt, kq, kq2, kl, ca, cb, cc, cd, ce, gs, gk, wl, hid, fs,
    part, mine, got1, got2, got3, acc, near, m32,
    zr, xrp, xrm, xo, zsr, zsl, xsp, xsm, fsp, fsm,
    ar, asd, azr, azsr, azsl, s1, r1, s2, r2, s3, r3, fsem, lsem, isem,
):
    dp = lax.axis_index("dp")
    tn = lax.axis_index("tensor")
    x = dp // NZ
    z = dp % NZ
    xp = (x + 1) % NX
    xm = (x + 3) % NX
    y = tn // 4
    zh = (tn // 2) % 2
    core = tn % 2

    def tensor_of(yy, zz, cc_):
        return (yy * 2 + zz) * 2 + cc_

    def rc(src, dst, ss, rs, xx, zz):
        return pltpu.make_async_remote_copy(
            src_ref=src, dst_ref=dst, send_sem=ss, recv_sem=rs,
            device_id=(xx * NZ + zz, tn), device_id_type=MESH,
        )

    def tc(src, dst, ss, rs, to):
        return pltpu.make_async_remote_copy(
            src_ref=src, dst_ref=dst, send_sem=ss, recv_sem=rs,
            device_id=(dp, to), device_id_type=MESH,
        )

    local = pltpu.make_async_copy(own, g.at[x, z], lsem)
    inputs = [
        pltpu.make_async_copy(src, dst, isem.at[i])
        for i, (src, dst) in enumerate(
            (
                (k_in, kb), (q_in, qb), (v_in, vb), (gate_in, gb), (decay_in, db), (rate_in, rate),
                (bias_in, bias), (gain_in, gain), (slot_in, slot), (weight_in, weight),
            )
        )
    ]

    bar = pltpu.get_barrier_semaphore()

    def sig(d, t):
        pl.semaphore_signal(bar, inc=1, device_id=(d, t), device_id_type=MESH)

    partner = tensor_of(y, zh, 1 - core)
    far = tensor_of(y, 1 - zh, core)
    sig(dp, far)
    sig(dp, tensor_of((y + 2) % 4, zh, core))
    sig(dp, tensor_of((y + 1) % 4, zh, core))
    sig(dp, tensor_of((y + 3) % 4, zh, core))
    sig(xp * NZ + z, tn)
    sig(xm * NZ + z, tn)

    @pl.when(z > 0)
    def _():
        sig(dp - 1, tn)

    @pl.when(z < NZ - 1)
    def _():
        sig(dp + 1, tn)

    sig(dp, partner)
    edge = jnp.logical_or(z == 0, z == NZ - 1)

    @pl.when(edge)
    def _():
        pl.semaphore_wait(bar, 8)

    @pl.when(jnp.logical_not(edge))
    def _():
        pl.semaphore_wait(bar, 9)

    def blk(xx, zp, h):
        return g.at[xx, zp, h, pl.ds(0, HEAD)]

    def z_right(zp, h, src):
        return rc(src, blk(x, zp, h), zsr.at[zp, h], zr.at[zp, h], x, z + 1)

    def z_left(zp, h, src):
        return rc(src, blk(x, zp, h), zsl.at[zp, h], zr.at[zp, h], x, z - 1)

    def x_plus(zp, h, src):
        return rc(src, blk(x, zp, h), xsp.at[zp, h], xrp.at[zp, h], xp, z)

    def x_minus(zp, h, src):
        return rc(src, blk(x, zp, h), xsm.at[zp, h], xrm.at[zp, h], xm, z)

    def f_plus(zp):
        return rc(blk(xm, zp, 0), blk(xm, zp, 0), fsp.at[zp], xo.at[zp, 0], xp, z)

    def f_minus(zp):
        return rc(blk(xp, zp, 1), blk(xp, zp, 1), fsm.at[zp], xo.at[zp, 1], xm, z)

    def tail(xx):
        return g.at[xx, z, :, pl.ds(HEAD, TAIL)]

    def tail_half(xx, h):
        return g.at[xx, z, h, pl.ds(HEAD, TAIL)]

    def t_plus(src):
        return rc(src, tail(x), asd.at[0], ar.at[0], xp, z)

    def t_minus(src):
        return rc(src, tail(x), asd.at[1], ar.at[1], xm, z)

    def tf_plus():
        return rc(tail_half(xm, 0), tail_half(xm, 0), asd.at[2], ar.at[2], xp, z)

    def tf_minus():
        return rc(tail_half(xp, 1), tail_half(xp, 1), asd.at[3], ar.at[3], xm, z)

    def tails(zp):
        return g.at[:, zp, :, pl.ds(HEAD, TAIL)]

    def tz_right(zp):
        return rc(tails(zp), tails(zp), azsr.at[zp], azr.at[zp], x, z + 1)

    def tz_left(zp):
        return rc(tails(zp), tails(zp), azsl.at[zp], azr.at[zp], x, z - 1)

    t_plus(own.at[:, pl.ds(HEAD, TAIL)]).start()
    t_minus(own.at[:, pl.ds(HEAD, TAIL)]).start()
    for h in range(2):
        src = own.at[h, pl.ds(0, HEAD)]

        @pl.when(z < NZ - 1)
        def _():
            z_right(z, h, src).start()

        @pl.when(z > 0)
        def _():
            z_left(z, h, src).start()

        x_plus(z, h, src).start()
        x_minus(z, h, src).start()
    local.start()
    for copy in inputs:
        copy.start()
    rc(tail(xm), tail(xm), asd.at[0], ar.at[0], xp, z).wait_recv()
    tf_plus().start()
    rc(tail(xp), tail(xp), asd.at[1], ar.at[1], xm, z).wait_recv()
    tf_minus().start()

    def prepare_keys():
        for copy in inputs:
            copy.wait()
        for src, dst in ((kb, k32), (qb, q32), (vb, v32), (gb, g32)):
            dst[...] = src[...].astype(F32)
        for n in range(STEPS * 2):
            dt[pl.ds(2 * n, 2), pl.ds(0, ROWS)] = db[n // 2, n % 2]
        for i in range(2 * STEPS):
            raw = k32[:, i, :] if i < STEPS else q32[:, i - STEPS, :]
            one = raw * lax.rsqrt(jnp.sum(raw * raw, axis=1, keepdims=True) + 1e-6)
            if i >= STEPS:
                one = one * (DK**-0.5)
            kq[i] = one
            high, low = split(one)
            kq2[pl.ds(i, ROWS, stride=16), :] = high
            kq2[pl.ds(i + 8, ROWS, stride=16), :] = low
            if i < STEPS:
                kl[pl.ds(i, ROWS, stride=16), :] = high
                kl[pl.ds(i + 4, ROWS, stride=16), :] = high
                kl[pl.ds(i + 8, ROWS, stride=16), :] = low
                kl[pl.ds(i + 12, ROWS, stride=16), :] = jnp.zeros_like(low)

    def prepare_gates():
        shape = (ROWS, DV)
        scalars = jnp.transpose(dt[...])
        keys = [kq[i] for i in range(2 * STEPS)]
        kk, kqd = {}, {}
        for s, t in PAIRS:
            if s < t:
                kk[s, t] = jnp.sum(keys[s] * keys[t], axis=1, keepdims=True)
            kqd[s, t] = jnp.sum(keys[s] * keys[STEPS + t], axis=1, keepdims=True)
        for h in range(HEADS):
            alpha = []
            for t in range(STEPS):
                d = scalars[0:ROWS, t * 4 + h : t * 4 + h + 1] + bias[h]
                soft = jnp.maximum(d, 0.0) + jnp.log1p(jnp.exp(-jnp.abs(d)))
                alpha.append(jnp.exp(-rate[h] * soft))
                b = scalars[0:ROWS, t * 4 + 2 + h : t * 4 + 3 + h]
                cb[h, t] = jnp.broadcast_to(1.0 / (1.0 + jnp.exp(-b)), shape)
            for t in range(STEPS):
                run = None
                for s in range(t, -1, -1):
                    n = PAIRS.index((s, t))
                    dot = kqd[s, t]
                    cd[h, n] = jnp.broadcast_to(dot if run is None else run * dot, shape)
                    if s < t:
                        cc[h, n] = jnp.broadcast_to(run * kk[s, t], shape)
                    if t == STEPS - 1:
                        ce[h, s] = jnp.broadcast_to(
                            jnp.ones_like(dot) if run is None else run, shape
                        )
                    run = alpha[s] if run is None else run * alpha[s]
                ca[h, t] = jnp.broadcast_to(run, shape)
                gate = g32[:, t, pl.ds(h * DV, DV)]
                gs[h, t] = gain[...] * gate / (1.0 + jnp.exp(-gate))

    def forward(zp):
        rc(blk(xm, zp, 0), blk(xm, zp, 0), fsp.at[zp], xrp.at[zp, 0], xp, z).wait_recv()
        f_plus(zp).start()
        rc(blk(xp, zp, 1), blk(xp, zp, 1), fsm.at[zp], xrm.at[zp, 1], xm, z).wait_recv()
        f_minus(zp).start()

    def gather_step(s, carry):
        zl = z - s
        zg = z + s
        for h in range(2):

            @pl.when(jnp.logical_and(s < NZ, zl >= 0))
            def _():
                z_right(zl, h, blk(x, zl, h)).wait_recv()

                @pl.when(z < NZ - 1)
                def _():
                    z_right(zl, h, blk(x, zl, h)).start()

                x_plus(zl, h, blk(x, zl, h)).start()
                x_minus(zl, h, blk(x, zl, h)).start()

            @pl.when(jnp.logical_and(s < NZ, zg < NZ))
            def _():
                z_left(zg, h, blk(x, zg, h)).wait_recv()

                @pl.when(z > 0)
                def _():
                    z_left(zg, h, blk(x, zg, h)).start()

                x_plus(zg, h, blk(x, zg, h)).start()
                x_minus(zg, h, blk(x, zg, h)).start()

        d = s - LAG_T

        @pl.when(d == 0)
        def _():
            rc(tail_half(x, 0), tail_half(x, 0), asd.at[2], ar.at[2], xp, z).wait_recv()
            rc(tail_half(x, 1), tail_half(x, 1), asd.at[3], ar.at[3], xm, z).wait_recv()
            local.wait()

            @pl.when(z < NZ - 1)
            def _():
                tz_right(z).start()

            @pl.when(z > 0)
            def _():
                tz_left(z).start()

        @pl.when(jnp.logical_and(d >= 1, z - d >= 0))
        def _():
            tz_right(z - d).wait_recv()

            @pl.when(z < NZ - 1)
            def _():
                tz_right(z - d).start()

        @pl.when(jnp.logical_and(d >= 1, z + d < NZ))
        def _():
            tz_left(z + d).wait_recv()

            @pl.when(z > 0)
            def _():
                tz_left(z + d).start()

        def onward(r, carry):
            both = jnp.minimum(z, NZ - 1 - z)
            paired = r <= 2 * both
            away = jnp.where(paired, (r + 1) // 2, r - both)
            below = jnp.where(paired, r % 2 == 1, z >= NZ // 2)
            forward(jnp.where(below, z - away, z + away))
            return carry

        def rank_at(quarter):
            return jnp.clip((quarter - FIRST + APART - 1 + 16 * APART) // APART - 16, 0, NZ)

        lax.fori_loop(rank_at(4 * s), rank_at(4 * s + 4), onward, 0)

        @pl.when(s == 1)
        def _():
            prepare_keys()

        @pl.when(s == 2)
        def _():
            prepare_gates()

        return carry

    lax.fori_loop(1, max(NZ + LAG_T, (FIRST + (NZ - 1) * APART) // 4 + 1), gather_step, 0)

    def last_blocks(zp, carry):
        rc(blk(xm, zp, 1), blk(xm, zp, 1), xsp.at[zp, 1], xrp.at[zp, 1], xp, z).wait_recv()
        rc(blk(xp, zp, 0), blk(xp, zp, 0), xsm.at[zp, 0], xrm.at[zp, 0], xm, z).wait_recv()
        f_plus(zp).wait_recv()
        f_minus(zp).wait_recv()
        return carry

    lax.fori_loop(0, NZ, last_blocks, 0)

    contract = (((1,), (1,)), ((), ()))

    def state_of(r):
        p = slot[r] // SAMPLES
        return g[p // (2 * NZ), (p // 2) % NZ, p % 2]

    def recall(r, carry):
        high, low = split(state_of(r))
        both = kq2[pl.ds(pl.multiple_of(r * 16, 16), 16), :].astype(BF16)
        a = lax.dot_general(both, high.astype(BF16), contract, preferred_element_type=F32)
        b = lax.dot_general(both, low.astype(BF16), contract, preferred_element_type=F32)
        total = a[0:8] + a[8:16] + b[0:8]
        at = pl.ds(pl.multiple_of(r * 8, 8), 8)
        gk[0, at, :] = total[:, 0:DV]
        gk[1, at, :] = total[:, DV:]
        return carry

    lax.fori_loop(0, ROWS, recall, 0, unroll=8)

    def run_steps(h, carry):
        lanes = pl.ds(pl.multiple_of(h * DV, DV), DV)
        u = []
        for t in range(STEPS):
            seen = ca[h, t] * gk[h, pl.ds(t, ROWS, stride=8), :]
            out = ca[h, t] * gk[h, pl.ds(STEPS + t, ROWS, stride=8), :]
            for s in range(t):
                seen = seen + cc[h, PAIRS.index((s, t))] * u[s]
            value = v32[:, t, lanes]
            u.append(cb[h, t] * (value - seen))
            for s in range(t + 1):
                out = out + cd[h, PAIRS.index((s, t))] * u[s]
            scale = lax.rsqrt(jnp.mean(out * out, axis=1, keepdims=True) + 1e-6)
            hid[pl.ds(t * ROWS, ROWS), lanes] = (out * scale * gs[h, t]).astype(BF16)
        for s in range(STEPS):
            high, low = split(ce[h, s] * u[s])
            wl[h, pl.ds(s, ROWS, stride=16), :] = high
            wl[h, pl.ds(s + 4, ROWS, stride=16), :] = low
            wl[h, pl.ds(s + 8, ROWS, stride=16), :] = high
            wl[h, pl.ds(s + 12, ROWS, stride=16), :] = jnp.zeros_like(high)
        return carry

    lax.fori_loop(0, HEADS, run_steps, 0)

    def cross(side, c, yy):
        at = (side, c, yy)
        return tc(part.at[at], got1.at[at], s1.at[at], r1.at[at], partner)

    def along_y(side, c, hop):
        at = (side, c, hop - 1)
        return tc(
            mine.at[side, c, (y + hop) % 4], got2.at[at], s2.at[at], r2.at[at],
            tensor_of((y + hop) % 4, zh, core),
        )

    def along_z(c):
        return tc(acc.at[c], got3.at[c], s3.at[c], r3.at[c], far)

    def product(n, carry):
        side = n // 4
        yy = (y + 1 + n) % 4
        zz = (zh + 1 + side) % 2
        at = pl.multiple_of((yy * 2 + zz) * 256, 256)
        both = jnp.dot(hid[...], weight[:, pl.ds(at, 256)], preferred_element_type=F32)
        theirs = jnp.where(core == 0, both[:, 128:], both[:, :128])
        ours = jnp.where(core == 0, both[:, :128], both[:, 128:])
        for c in range(CHUNKS):
            part[side, c, yy] = theirs[c * CROWS : (c + 1) * CROWS]
            mine[side, c, yy] = ours[c * CROWS : (c + 1) * CROWS]
            cross(side, c, yy).start()
        return carry

    lax.fori_loop(0, 8, product, 0)

    def merge(n, carry):
        side = n // (4 * CHUNKS)
        c = (n // 4) % CHUNKS
        hop = (n + 1) % 4
        yy = (y + hop) % 4
        cross(side, c, yy).wait_recv()
        mine[side, c, yy] = mine[side, c, yy] + got1[side, c, yy]

        @pl.when(hop > 0)
        def _():
            along_y(side, c, hop).start()

        return carry

    lax.fori_loop(0, 8 * CHUNKS, merge, 0)

    def summed(side, c):
        for hop in (1, 2, 3):
            along_y(side, c, hop).wait_recv()
        return mine[side, c, y] + got2[side, c, 0] + got2[side, c, 1] + got2[side, c, 2]

    def send_z(c, carry):
        acc[c] = summed(0, c)
        along_z(c).start()
        return carry

    lax.fori_loop(0, CHUNKS, send_z, 0)

    def finish(r, carry):
        state = state_of(r)
        at = pl.ds(pl.multiple_of(r * 16, 16), 16)
        keys = kl[at, :].astype(BF16)
        for h in range(HEADS):
            update = lax.dot_general(
                wl[h, at, :].astype(BF16), keys, (((0,), (0,)), ((), ())),
                preferred_element_type=F32,
            )
            decay = ca[h, STEPS - 1, pl.ds(r, 1), :]
            fs[r, pl.ds(h * DV, DV), :] = (
                decay * state[h * DV : (h + 1) * DV] + update
            ).astype(BF16)
        return carry

    def write(i):
        some = pl.ds(i * (ROWS // 2), ROWS // 2)
        return pltpu.make_async_copy(fs.at[some], final.at[some], fsem.at[i])

    def half(i, carry):
        lax.fori_loop(i * (ROWS // 2), (i + 1) * (ROWS // 2), finish, 0)
        write(i).start()
        return carry

    lax.fori_loop(0, 2, half, 0)

    t_plus(tail(x)).wait_send()
    t_minus(tail(x)).wait_send()
    tf_plus().wait_send()
    tf_minus().wait_send()

    def sent(zp, carry):
        for h in range(2):
            x_plus(zp, h, blk(x, zp, h)).wait_send()
            x_minus(zp, h, blk(x, zp, h)).wait_send()

            @pl.when(jnp.logical_and(z < NZ - 1, zp <= z))
            def _():
                z_right(zp, h, blk(x, zp, h)).wait_send()

            @pl.when(jnp.logical_and(z > 0, zp >= z))
            def _():
                z_left(zp, h, blk(x, zp, h)).wait_send()

        @pl.when(jnp.logical_and(z < NZ - 1, zp <= z))
        def _():
            tz_right(zp).wait_send()

        @pl.when(jnp.logical_and(z > 0, zp >= z))
        def _():
            tz_left(zp).wait_send()

        f_plus(zp).wait_send()
        f_minus(zp).wait_send()
        return carry

    lax.fori_loop(0, NZ, sent, 0)

    def left(n, carry):
        for yy in range(4):
            cross(n // CHUNKS, n % CHUNKS, yy).wait_send()
        for hop in (1, 2, 3):
            along_y(n // CHUNKS, n % CHUNKS, hop).wait_send()
        return carry

    lax.fori_loop(0, 2 * CHUNKS, left, 0)

    def keep(c, carry):
        near[c] = summed(1, c)
        return carry

    lax.fori_loop(0, CHUNKS, keep, 0)

    def gather_z(c, carry):
        along_z(c).wait_recv()
        for i in range(STEPS // CHUNKS):
            some = pl.ds(i * ROWS, ROWS)
            m32[:, c * (STEPS // CHUNKS) + i, :] = near[c, some] + got3[c, some]
        return carry

    lax.fori_loop(0, CHUNKS, gather_z, 0)
    mixed[...] = m32[...].astype(BF16)

    for c in range(CHUNKS):
        along_z(c).wait_send()
    write(0).wait()
    write(1).wait()


def hand_over(mixed_in, final_in, mixed, final, held, kept, sem):
    size = ROWS // PIECES
    pieces = [pl.ds(i * size, size) for i in range(PIECES)]
    reads = [pltpu.make_async_copy(final_in.at[p], held.at[p], sem.at[i]) for i, p in enumerate(pieces)]
    reads.append(pltpu.make_async_copy(mixed_in, kept, sem.at[PIECES]))
    writes = [
        pltpu.make_async_copy(held.at[p], final.at[p], sem.at[PIECES + 1 + i])
        for i, p in enumerate(pieces)
    ]
    writes.append(pltpu.make_async_copy(kept, mixed, sem.at[2 * PIECES + 1]))
    for read in reads:
        read.start()
    for read, write in zip(reads, writes):
        read.wait()
        write.start()
    for write in writes:
        write.wait()


def body(
    owner_states, sample_slot, query_in, key_in, value_in, gate_in, decay_in,
    decay_rate, dt_bias, norm_gain, out_weight,
):
    vmem = pl.BlockSpec(memory_space=pltpu.VMEM)
    hbm = pl.BlockSpec(memory_space=pltpu.HBM)
    dma = pltpu.SemaphoreType.DMA
    npair = len(PAIRS)
    mixed, final = pl.pallas_call(
        kernel,
        out_shape=(
            jax.ShapeDtypeStruct((ROWS, STEPS, 128), BF16),
            jax.ShapeDtypeStruct((ROWS, HEADS * DV, DK), BF16),
        ),
        in_specs=[hbm] * 11,
        out_specs=(vmem, hbm),
        scratch_shapes=[
            pltpu.SMEM((ROWS,), jnp.int32),
            pltpu.VMEM((ROWS, STEPS, DK), BF16),
            pltpu.VMEM((ROWS, STEPS, DK), BF16),
            pltpu.VMEM((ROWS, STEPS, HEADS * DV), BF16),
            pltpu.VMEM((ROWS, STEPS, HEADS * DV), BF16),
            pltpu.VMEM((STEPS, 2, HEADS, ROWS), F32),
            pltpu.SMEM((HEADS,), F32),
            pltpu.SMEM((HEADS,), F32),
            pltpu.VMEM((1, DV), F32),
            pltpu.VMEM((HEADS * DV, 2048), BF16),
            pltpu.VMEM((NX, NZ, 2, HEADS * DV, DK), F32),
            pltpu.VMEM((ROWS, STEPS, DK), F32),
            pltpu.VMEM((ROWS, STEPS, DK), F32),
            pltpu.VMEM((ROWS, STEPS, HEADS * DV), F32),
            pltpu.VMEM((ROWS, STEPS, HEADS * DV), F32),
            pltpu.VMEM((STEPS * 2 * HEADS, 128), F32),
            pltpu.VMEM((2 * STEPS, ROWS, DK), F32),
            pltpu.VMEM((ROWS * 16, DK), F32),
            pltpu.VMEM((ROWS * 16, DK), F32),
            pltpu.VMEM((HEADS, STEPS, ROWS, DV), F32),
            pltpu.VMEM((HEADS, STEPS, ROWS, DV), F32),
            pltpu.VMEM((HEADS, npair, ROWS, DV), F32),
            pltpu.VMEM((HEADS, npair, ROWS, DV), F32),
            pltpu.VMEM((HEADS, STEPS, ROWS, DV), F32),
            pltpu.VMEM((HEADS, STEPS, ROWS, DV), F32),
            pltpu.VMEM((HEADS, ROWS * 8, DV), F32),
            pltpu.VMEM((HEADS, ROWS * 16, DV), F32),
            pltpu.VMEM((ROWS * STEPS, HEADS * DV), BF16),
            pltpu.VMEM((ROWS, HEADS * DV, DK), BF16),
            pltpu.VMEM((2, CHUNKS, 4, CROWS, 128), F32),
            pltpu.VMEM((2, CHUNKS, 4, CROWS, 128), F32),
            pltpu.VMEM((2, CHUNKS, 4, CROWS, 128), F32),
            pltpu.VMEM((2, CHUNKS, 3, CROWS, 128), F32),
            pltpu.VMEM((CHUNKS, CROWS, 128), F32),
            pltpu.VMEM((CHUNKS, CROWS, 128), F32),
            pltpu.VMEM((CHUNKS, CROWS, 128), F32),
            pltpu.VMEM((ROWS, STEPS, 128), F32),
        ]
        + [dma((NZ, 2)) for _ in range(8)]
        + [dma((NZ,)), dma((NZ,)), dma((4,)), dma((4,)), dma((NZ,)), dma((NZ,)), dma((NZ,))]
        + [dma((2, CHUNKS, 4)), dma((2, CHUNKS, 4)), dma((2, CHUNKS, 3)), dma((2, CHUNKS, 3))]
        + [dma((CHUNKS,)), dma((CHUNKS,)), dma((2,)), dma, dma((10,))],
        compiler_params=pltpu.CompilerParams(
            collective_id=0, has_side_effects=True, vmem_limit_bytes=56 * 2**20
        ),
    )(
        owner_states.reshape(2, HEADS * DV, DK),
        sample_slot,
        query_in,
        key_in,
        value_in,
        gate_in,
        decay_in.transpose(1, 2, 3, 0),
        decay_rate,
        dt_bias,
        norm_gain.reshape(1, DV),
        out_weight,
    )
    mixed, final = pl.pallas_call(
        hand_over,
        out_shape=(
            jax.ShapeDtypeStruct((ROWS, STEPS, 128), BF16),
            jax.ShapeDtypeStruct((ROWS, HEADS * DV, DK), BF16),
        ),
        in_specs=[hbm, hbm],
        out_specs=(hbm, hbm),
        scratch_shapes=[
            pltpu.VMEM((ROWS, HEADS * DV, DK), BF16),
            pltpu.VMEM((ROWS, STEPS, 128), BF16),
            dma((2 * PIECES + 2,)),
        ],
        compiler_params=pltpu.CompilerParams(vmem_limit_bytes=56 * 2**20),
    )(mixed, final)
    return mixed, final.reshape(ROWS, HEADS, DV, DK)


def solution(mesh):
    return jax.shard_map(
        body,
        mesh=mesh,
        in_specs=(
            P("dp", "tensor", None, None),
            P("dp"),
            P("dp", None, "tensor"),
            P("dp", None, "tensor"),
            P("dp", None, "tensor"),
            P("dp", None, "tensor"),
            P("dp", None, None, "tensor"),
            P("tensor"),
            P("tensor"),
            P(),
            P("tensor", None),
        ),
        out_specs=(P("dp", None, "tensor"), P("dp", "tensor", None, None)),
        check_vma=False,
    )
```

```python
import functools

import jax
import jax.numpy as jnp
from jax import lax
from jax.experimental import pallas as pl
from jax.experimental.pallas import tpu as pltpu
from jax.sharding import PartitionSpec as P

MESH = pl.DeviceIdType.MESH
F32 = jnp.float32
BF16 = jnp.bfloat16
NX, NZ = 4, 8
ROWS, STEPS, DK, DV, HEADS = 32, 4, 128, 128, 2
SAMPLES = 16
TAIL = 40
HEAD = HEADS * DV - TAIL
FIRST, APART = 14, 3
LAG_T = 3
CHUNKS = 2
PIECES = 4
CROWS = ROWS * STEPS // CHUNKS
PAIRS = [(s, t) for t in range(STEPS) for s in range(t + 1)]


def split(value):
    high = value.astype(BF16).astype(F32)
    return high, value - high


def kernel(
    own, slot_in, q_in, k_in, v_in, gate_in, decay_in, rate_in, bias_in, gain_in, weight_in,
    mixed, final,
    slot, qb, kb, vb, gb, db, rate, bias, gain, weight,
    g, q32, k32, v32, g32, dt, kq, kq2, kl, ca, cb, cc, cd, ce, gs, gk, wl, hid,
    part, mine, got1, got2, got3, acc, near, m32,
    zr, xrp, xrm, xo, zsr, zsl, xsp, xsm, fsp, fsm,
    ar, asd, azr, azsr, azsl, s1, r1, s2, r2, s3, r3, lsem, isem, far_in,
):
    dp = lax.axis_index("dp")
    tn = lax.axis_index("tensor")
    x = dp // NZ
    z = dp % NZ
    xp = (x + 1) % NX
    xm = (x + 3) % NX
    y = tn // 4
    zh = (tn // 2) % 2
    core = tn % 2

    def tensor_of(yy, zz, cc_):
        return (yy * 2 + zz) * 2 + cc_

    def rc(src, dst, ss, rs, xx, zz):
        return pltpu.make_async_remote_copy(
            src_ref=src, dst_ref=dst, send_sem=ss, recv_sem=rs,
            device_id=(xx * NZ + zz, tn), device_id_type=MESH,
        )

    def tc(src, dst, ss, rs, to):
        return pltpu.make_async_remote_copy(
            src_ref=src, dst_ref=dst, send_sem=ss, recv_sem=rs,
            device_id=(dp, to), device_id_type=MESH,
        )

    local = pltpu.make_async_copy(own, g.at[x, z], lsem)
    inputs = [
        pltpu.make_async_copy(src, dst, isem.at[i])
        for i, (src, dst) in enumerate(
            (
                (k_in, kb), (q_in, qb), (v_in, vb), (gate_in, gb), (decay_in, db), (rate_in, rate),
                (bias_in, bias), (gain_in, gain), (slot_in, slot), (weight_in, weight),
            )
        )
    ]

    bar = pltpu.get_barrier_semaphore()

    def sig(d, t):
        pl.semaphore_signal(bar, inc=1, device_id=(d, t), device_id_type=MESH)

    partner = tensor_of(y, zh, 1 - core)
    far = tensor_of(y, 1 - zh, core)

    @pl.when(zh == 0)
    def _():
        sig(dp, far)

    sig(dp, tensor_of((y + 2) % 4, zh, core))
    sig(dp, tensor_of((y + 1) % 4, zh, core))
    sig(dp, tensor_of((y + 3) % 4, zh, core))
    sig(xp * NZ + z, tn)
    sig(xm * NZ + z, tn)

    @pl.when(z > 0)
    def _():
        sig(dp - 1, tn)

    @pl.when(z < NZ - 1)
    def _():
        sig(dp + 1, tn)

    sig(dp, partner)
    edge = jnp.logical_or(z == 0, z == NZ - 1)

    @pl.when(jnp.logical_and(edge, zh == 0))
    def _():
        pl.semaphore_wait(bar, 7)

    @pl.when(jnp.logical_xor(edge, zh == 0))
    def _():
        pl.semaphore_wait(bar, 8)

    @pl.when(jnp.logical_and(jnp.logical_not(edge), zh == 1))
    def _():
        pl.semaphore_wait(bar, 9)

    @pl.when(zh == 1)
    def _():
        pl.semaphore_signal(far_in, inc=1, device_id=(dp, far), device_id_type=MESH)

    def blk(xx, zp, h):
        return g.at[xx, zp, h, pl.ds(0, HEAD)]

    def z_right(zp, h, src):
        return rc(src, blk(x, zp, h), zsr.at[zp, h], zr.at[zp, h], x, z + 1)

    def z_left(zp, h, src):
        return rc(src, blk(x, zp, h), zsl.at[zp, h], zr.at[zp, h], x, z - 1)

    def x_plus(zp, h, src):
        return rc(src, blk(x, zp, h), xsp.at[zp, h], xrp.at[zp, h], xp, z)

    def x_minus(zp, h, src):
        return rc(src, blk(x, zp, h), xsm.at[zp, h], xrm.at[zp, h], xm, z)

    def f_plus(zp):
        return rc(blk(xm, zp, 0), blk(xm, zp, 0), fsp.at[zp], xo.at[zp, 0], xp, z)

    def f_minus(zp):
        return rc(blk(xp, zp, 1), blk(xp, zp, 1), fsm.at[zp], xo.at[zp, 1], xm, z)

    def tail(xx):
        return g.at[xx, z, :, pl.ds(HEAD, TAIL)]

    def tail_half(xx, h):
        return g.at[xx, z, h, pl.ds(HEAD, TAIL)]

    def t_plus(src):
        return rc(src, tail(x), asd.at[0], ar.at[0], xp, z)

    def t_minus(src):
        return rc(src, tail(x), asd.at[1], ar.at[1], xm, z)

    def tf_plus():
        return rc(tail_half(xm, 0), tail_half(xm, 0), asd.at[2], ar.at[2], xp, z)

    def tf_minus():
        return rc(tail_half(xp, 1), tail_half(xp, 1), asd.at[3], ar.at[3], xm, z)

    def tails(zp):
        return g.at[:, zp, :, pl.ds(HEAD, TAIL)]

    def tz_right(zp):
        return rc(tails(zp), tails(zp), azsr.at[zp], azr.at[zp], x, z + 1)

    def tz_left(zp):
        return rc(tails(zp), tails(zp), azsl.at[zp], azr.at[zp], x, z - 1)

    t_plus(own.at[:, pl.ds(HEAD, TAIL)]).start()
    t_minus(own.at[:, pl.ds(HEAD, TAIL)]).start()
    for h in range(2):
        src = own.at[h, pl.ds(0, HEAD)]

        @pl.when(z < NZ - 1)
        def _():
            z_right(z, h, src).start()

        @pl.when(z > 0)
        def _():
            z_left(z, h, src).start()

        x_plus(z, h, src).start()
        x_minus(z, h, src).start()
    local.start()
    for copy in inputs:
        copy.start()
    rc(tail(xm), tail(xm), asd.at[0], ar.at[0], xp, z).wait_recv()
    tf_plus().start()
    rc(tail(xp), tail(xp), asd.at[1], ar.at[1], xm, z).wait_recv()
    tf_minus().start()

    def prepare_keys():
        for copy in inputs:
            copy.wait()
        for src, dst in ((kb, k32), (qb, q32), (vb, v32), (gb, g32)):
            dst[...] = src[...].astype(F32)
        for n in range(STEPS * 2):
            dt[pl.ds(2 * n, 2), pl.ds(0, ROWS)] = db[n // 2, n % 2]
        for i in range(2 * STEPS):
            raw = k32[:, i, :] if i < STEPS else q32[:, i - STEPS, :]
            one = raw * lax.rsqrt(jnp.sum(raw * raw, axis=1, keepdims=True) + 1e-6)
            if i >= STEPS:
                one = one * (DK**-0.5)
            kq[i] = one
            high, low = split(one)
            kq2[pl.ds(i, ROWS, stride=16), :] = high
            kq2[pl.ds(i + 8, ROWS, stride=16), :] = low
            if i < STEPS:
                kl[pl.ds(i, ROWS, stride=16), :] = high
                kl[pl.ds(i + 4, ROWS, stride=16), :] = high
                kl[pl.ds(i + 8, ROWS, stride=16), :] = low
                kl[pl.ds(i + 12, ROWS, stride=16), :] = jnp.zeros_like(low)

    def prepare_gates():
        shape = (ROWS, DV)
        scalars = jnp.transpose(dt[...])
        keys = [kq[i] for i in range(2 * STEPS)]
        kk, kqd = {}, {}
        for s, t in PAIRS:
            if s < t:
                kk[s, t] = jnp.sum(keys[s] * keys[t], axis=1, keepdims=True)
            kqd[s, t] = jnp.sum(keys[s] * keys[STEPS + t], axis=1, keepdims=True)
        for h in range(HEADS):
            alpha = []
            for t in range(STEPS):
                d = scalars[0:ROWS, t * 4 + h : t * 4 + h + 1] + bias[h]
                soft = jnp.maximum(d, 0.0) + jnp.log1p(jnp.exp(-jnp.abs(d)))
                alpha.append(jnp.exp(-rate[h] * soft))
                b = scalars[0:ROWS, t * 4 + 2 + h : t * 4 + 3 + h]
                cb[h, t] = jnp.broadcast_to(1.0 / (1.0 + jnp.exp(-b)), shape)
            for t in range(STEPS):
                run = None
                for s in range(t, -1, -1):
                    n = PAIRS.index((s, t))
                    dot = kqd[s, t]
                    cd[h, n] = jnp.broadcast_to(dot if run is None else run * dot, shape)
                    if s < t:
                        cc[h, n] = jnp.broadcast_to(run * kk[s, t], shape)
                    if t == STEPS - 1:
                        ce[h, s] = jnp.broadcast_to(
                            jnp.ones_like(dot) if run is None else run, shape
                        )
                    run = alpha[s] if run is None else run * alpha[s]
                ca[h, t] = jnp.broadcast_to(run, shape)
                gate = g32[:, t, pl.ds(h * DV, DV)]
                gs[h, t] = gain[...] * gate / (1.0 + jnp.exp(-gate))

    def forward(zp):
        rc(blk(xm, zp, 0), blk(xm, zp, 0), fsp.at[zp], xrp.at[zp, 0], xp, z).wait_recv()
        f_plus(zp).start()
        rc(blk(xp, zp, 1), blk(xp, zp, 1), fsm.at[zp], xrm.at[zp, 1], xm, z).wait_recv()
        f_minus(zp).start()

    def gather_step(s, carry):
        zl = z - s
        zg = z + s
        for h in range(2):

            @pl.when(jnp.logical_and(s < NZ, zl >= 0))
            def _():
                z_right(zl, h, blk(x, zl, h)).wait_recv()

                @pl.when(z < NZ - 1)
                def _():
                    z_right(zl, h, blk(x, zl, h)).start()

                x_plus(zl, h, blk(x, zl, h)).start()
                x_minus(zl, h, blk(x, zl, h)).start()

            @pl.when(jnp.logical_and(s < NZ, zg < NZ))
            def _():
                z_left(zg, h, blk(x, zg, h)).wait_recv()

                @pl.when(z > 0)
                def _():
                    z_left(zg, h, blk(x, zg, h)).start()

                x_plus(zg, h, blk(x, zg, h)).start()
                x_minus(zg, h, blk(x, zg, h)).start()

        d = s - LAG_T

        @pl.when(d == 0)
        def _():
            rc(tail_half(x, 0), tail_half(x, 0), asd.at[2], ar.at[2], xp, z).wait_recv()
            rc(tail_half(x, 1), tail_half(x, 1), asd.at[3], ar.at[3], xm, z).wait_recv()
            local.wait()

            @pl.when(z < NZ - 1)
            def _():
                tz_right(z).start()

            @pl.when(z > 0)
            def _():
                tz_left(z).start()

        @pl.when(jnp.logical_and(d >= 1, z - d >= 0))
        def _():
            tz_right(z - d).wait_recv()

            @pl.when(z < NZ - 1)
            def _():
                tz_right(z - d).start()

        @pl.when(jnp.logical_and(d >= 1, z + d < NZ))
        def _():
            tz_left(z + d).wait_recv()

            @pl.when(z > 0)
            def _():
                tz_left(z + d).start()

        def onward(r, carry):
            both = jnp.minimum(z, NZ - 1 - z)
            paired = r <= 2 * both
            away = jnp.where(paired, (r + 1) // 2, r - both)
            below = jnp.where(paired, r % 2 == 1, z >= NZ // 2)
            forward(jnp.where(below, z - away, z + away))
            return carry

        def rank_at(quarter):
            return jnp.clip((quarter - FIRST + APART - 1 + 16 * APART) // APART - 16, 0, NZ)

        lax.fori_loop(rank_at(4 * s), rank_at(4 * s + 4), onward, 0)

        @pl.when(s == 1)
        def _():
            prepare_keys()

        @pl.when(s == 2)
        def _():
            prepare_gates()

        return carry

    lax.fori_loop(1, max(NZ + LAG_T, (FIRST + (NZ - 1) * APART) // 4 + 1), gather_step, 0)

    def last_blocks(zp, carry):
        rc(blk(xm, zp, 1), blk(xm, zp, 1), xsp.at[zp, 1], xrp.at[zp, 1], xp, z).wait_recv()
        rc(blk(xp, zp, 0), blk(xp, zp, 0), xsm.at[zp, 0], xrm.at[zp, 0], xm, z).wait_recv()
        f_plus(zp).wait_recv()
        f_minus(zp).wait_recv()
        return carry

    lax.fori_loop(0, NZ, last_blocks, 0)

    contract = (((1,), (1,)), ((), ()))

    def state_of(r):
        p = slot[r] // SAMPLES
        return g[p // (2 * NZ), (p // 2) % NZ, p % 2]

    def recall(r, carry):
        high, low = split(state_of(r))
        both = kq2[pl.ds(pl.multiple_of(r * 16, 16), 16), :].astype(BF16)
        a = lax.dot_general(both, high.astype(BF16), contract, preferred_element_type=F32)
        b = lax.dot_general(both, low.astype(BF16), contract, preferred_element_type=F32)
        total = a[0:8] + a[8:16] + b[0:8]
        at = pl.ds(pl.multiple_of(r * 8, 8), 8)
        gk[0, at, :] = total[:, 0:DV]
        gk[1, at, :] = total[:, DV:]
        return carry

    lax.fori_loop(0, ROWS, recall, 0, unroll=8)

    def run_steps(h, carry):
        lanes = pl.ds(pl.multiple_of(h * DV, DV), DV)
        u = []
        for t in range(STEPS):
            seen = ca[h, t] * gk[h, pl.ds(t, ROWS, stride=8), :]
            out = ca[h, t] * gk[h, pl.ds(STEPS + t, ROWS, stride=8), :]
            for s in range(t):
                seen = seen + cc[h, PAIRS.index((s, t))] * u[s]
            value = v32[:, t, lanes]
            u.append(cb[h, t] * (value - seen))
            for s in range(t + 1):
                out = out + cd[h, PAIRS.index((s, t))] * u[s]
            scale = lax.rsqrt(jnp.mean(out * out, axis=1, keepdims=True) + 1e-6)
            hid[pl.ds(t * ROWS, ROWS), lanes] = (out * scale * gs[h, t]).astype(BF16)
        for s in range(STEPS):
            high, low = split(ce[h, s] * u[s])
            wl[h, pl.ds(s, ROWS, stride=16), :] = high
            wl[h, pl.ds(s + 4, ROWS, stride=16), :] = low
            wl[h, pl.ds(s + 8, ROWS, stride=16), :] = high
            wl[h, pl.ds(s + 12, ROWS, stride=16), :] = jnp.zeros_like(high)
        return carry

    lax.fori_loop(0, HEADS, run_steps, 0)

    def cross(side, c, yy):
        at = (side, c, yy)
        return tc(part.at[at], got1.at[at], s1.at[at], r1.at[at], partner)

    def along_y(side, c, hop):
        at = (side, c, hop - 1)
        return tc(
            mine.at[side, c, (y + hop) % 4], got2.at[at], s2.at[at], r2.at[at],
            tensor_of((y + hop) % 4, zh, core),
        )

    def along_z(c):
        return tc(acc.at[c], got3.at[c], s3.at[c], r3.at[c], far)

    def product(n, carry):
        side = n // 4
        yy = (y + 1 + n) % 4
        zz = (zh + 1 + side) % 2
        at = pl.multiple_of((yy * 2 + zz) * 256, 256)
        both = jnp.dot(hid[...], weight[:, pl.ds(at, 256)], preferred_element_type=F32)
        theirs = jnp.where(core == 0, both[:, 128:], both[:, :128])
        ours = jnp.where(core == 0, both[:, :128], both[:, 128:])
        for c in range(CHUNKS):
            part[side, c, yy] = theirs[c * CROWS : (c + 1) * CROWS]
            mine[side, c, yy] = ours[c * CROWS : (c + 1) * CROWS]
            cross(side, c, yy).start()
        return carry

    lax.fori_loop(0, 8, product, 0)

    def merge(n, carry):
        side = n // (4 * CHUNKS)
        c = (n // 4) % CHUNKS
        hop = (n + 1) % 4
        yy = (y + hop) % 4
        cross(side, c, yy).wait_recv()
        mine[side, c, yy] = mine[side, c, yy] + got1[side, c, yy]

        @pl.when(hop > 0)
        def _():
            along_y(side, c, hop).start()

        return carry

    lax.fori_loop(0, 8 * CHUNKS, merge, 0)

    def summed(side, c):
        for hop in (1, 2, 3):
            along_y(side, c, hop).wait_recv()
        return mine[side, c, y] + got2[side, c, 0] + got2[side, c, 1] + got2[side, c, 2]

    @pl.when(zh == 0)
    def _():
        pl.semaphore_wait(far_in, 1)

    def send_z(c, carry):
        acc[c] = summed(0, c)
        along_z(c).start()
        return carry

    lax.fori_loop(0, CHUNKS, send_z, 0)

    def finish(r, carry):
        state = state_of(r)
        at = pl.ds(pl.multiple_of(r * 16, 16), 16)
        keys = kl[at, :].astype(BF16)
        for h in range(HEADS):
            update = lax.dot_general(
                wl[h, at, :].astype(BF16), keys, (((0,), (0,)), ((), ())),
                preferred_element_type=F32,
            )
            decay = ca[h, STEPS - 1, pl.ds(r, 1), :]
            final[r, pl.ds(h * DV, DV), :] = (
                decay * state[h * DV : (h + 1) * DV] + update
            ).astype(BF16)
        return carry

    lax.fori_loop(0, ROWS, finish, 0)

    t_plus(tail(x)).wait_send()
    t_minus(tail(x)).wait_send()
    tf_plus().wait_send()
    tf_minus().wait_send()

    def sent(zp, carry):
        for h in range(2):
            x_plus(zp, h, blk(x, zp, h)).wait_send()
            x_minus(zp, h, blk(x, zp, h)).wait_send()

            @pl.when(jnp.logical_and(z < NZ - 1, zp <= z))
            def _():
                z_right(zp, h, blk(x, zp, h)).wait_send()

            @pl.when(jnp.logical_and(z > 0, zp >= z))
            def _():
                z_left(zp, h, blk(x, zp, h)).wait_send()

        @pl.when(jnp.logical_and(z < NZ - 1, zp <= z))
        def _():
            tz_right(zp).wait_send()

        @pl.when(jnp.logical_and(z > 0, zp >= z))
        def _():
            tz_left(zp).wait_send()

        f_plus(zp).wait_send()
        f_minus(zp).wait_send()
        return carry

    lax.fori_loop(0, NZ, sent, 0)

    def left(n, carry):
        for yy in range(4):
            cross(n // CHUNKS, n % CHUNKS, yy).wait_send()
        for hop in (1, 2, 3):
            along_y(n // CHUNKS, n % CHUNKS, hop).wait_send()
        return carry

    lax.fori_loop(0, 2 * CHUNKS, left, 0)

    def keep(c, carry):
        near[c] = summed(1, c)
        return carry

    lax.fori_loop(0, CHUNKS, keep, 0)

    def gather_z(c, carry):
        along_z(c).wait_recv()
        for i in range(STEPS // CHUNKS):
            some = pl.ds(i * ROWS, ROWS)
            m32[:, c * (STEPS // CHUNKS) + i, :] = near[c, some] + got3[c, some]
        return carry

    lax.fori_loop(0, CHUNKS, gather_z, 0)
    mixed[...] = m32[...].astype(BF16)

    for c in range(CHUNKS):
        along_z(c).wait_send()


def hand_over(mixed_in, final_in, mixed, final, sem):
    size = ROWS // PIECES
    copies = [
        pltpu.make_async_copy(final_in.at[pl.ds(i * size, size)], final.at[pl.ds(i * size, size)], sem.at[i])
        for i in range(PIECES)
    ]
    copies.append(pltpu.make_async_copy(mixed_in, mixed, sem.at[PIECES]))
    for copy in copies:
        copy.start()
    for copy in copies:
        copy.wait()


def body(
    owner_states, sample_slot, query_in, key_in, value_in, gate_in, decay_in,
    decay_rate, dt_bias, norm_gain, out_weight,
):
    vmem = pl.BlockSpec(memory_space=pltpu.VMEM)
    hbm = pl.BlockSpec(memory_space=pltpu.HBM)
    dma = pltpu.SemaphoreType.DMA
    npair = len(PAIRS)
    operands = [
        pltpu.with_memory_space_constraint(value, pltpu.HBM)
        for value in (
            owner_states.reshape(2, HEADS * DV, DK),
            sample_slot,
            query_in,
            key_in,
            value_in,
            gate_in,
            decay_in.transpose(1, 2, 3, 0),
            decay_rate,
            dt_bias,
            norm_gain.reshape(1, DV),
            out_weight,
        )
    ]
    mixed, final = pl.pallas_call(
        kernel,
        out_shape=(
            pltpu.VMEM((ROWS, STEPS, 128), BF16),
            pltpu.VMEM((ROWS, HEADS * DV, DK), BF16),
        ),
        in_specs=[hbm] * 11,
        out_specs=(vmem, vmem),
        scratch_shapes=[
            pltpu.SMEM((ROWS,), jnp.int32),
            pltpu.VMEM((ROWS, STEPS, DK), BF16),
            pltpu.VMEM((ROWS, STEPS, DK), BF16),
            pltpu.VMEM((ROWS, STEPS, HEADS * DV), BF16),
            pltpu.VMEM((ROWS, STEPS, HEADS * DV), BF16),
            pltpu.VMEM((STEPS, 2, HEADS, ROWS), F32),
            pltpu.SMEM((HEADS,), F32),
            pltpu.SMEM((HEADS,), F32),
            pltpu.VMEM((1, DV), F32),
            pltpu.VMEM((HEADS * DV, 2048), BF16),
            pltpu.VMEM((NX, NZ, 2, HEADS * DV, DK), F32),
            pltpu.VMEM((ROWS, STEPS, DK), F32),
            pltpu.VMEM((ROWS, STEPS, DK), F32),
            pltpu.VMEM((ROWS, STEPS, HEADS * DV), F32),
            pltpu.VMEM((ROWS, STEPS, HEADS * DV), F32),
            pltpu.VMEM((STEPS * 2 * HEADS, 128), F32),
            pltpu.VMEM((2 * STEPS, ROWS, DK), F32),
            pltpu.VMEM((ROWS * 16, DK), F32),
            pltpu.VMEM((ROWS * 16, DK), F32),
            pltpu.VMEM((HEADS, STEPS, ROWS, DV), F32),
            pltpu.VMEM((HEADS, STEPS, ROWS, DV), F32),
            pltpu.VMEM((HEADS, npair, ROWS, DV), F32),
            pltpu.VMEM((HEADS, npair, ROWS, DV), F32),
            pltpu.VMEM((HEADS, STEPS, ROWS, DV), F32),
            pltpu.VMEM((HEADS, STEPS, ROWS, DV), F32),
            pltpu.VMEM((HEADS, ROWS * 8, DV), F32),
            pltpu.VMEM((HEADS, ROWS * 16, DV), F32),
            pltpu.VMEM((ROWS * STEPS, HEADS * DV), BF16),
            pltpu.VMEM((2, CHUNKS, 4, CROWS, 128), F32),
            pltpu.VMEM((2, CHUNKS, 4, CROWS, 128), F32),
            pltpu.VMEM((2, CHUNKS, 4, CROWS, 128), F32),
            pltpu.VMEM((2, CHUNKS, 3, CROWS, 128), F32),
            pltpu.VMEM((CHUNKS, CROWS, 128), F32),
            pltpu.VMEM((CHUNKS, CROWS, 128), F32),
            pltpu.VMEM((CHUNKS, CROWS, 128), F32),
            pltpu.VMEM((ROWS, STEPS, 128), F32),
        ]
        + [dma((NZ, 2)) for _ in range(8)]
        + [dma((NZ,)), dma((NZ,)), dma((4,)), dma((4,)), dma((NZ,)), dma((NZ,)), dma((NZ,))]
        + [dma((2, CHUNKS, 4)), dma((2, CHUNKS, 4)), dma((2, CHUNKS, 3)), dma((2, CHUNKS, 3))]
        + [dma((CHUNKS,)), dma((CHUNKS,)), dma, dma((10,)), pltpu.SemaphoreType.REGULAR],
        compiler_params=pltpu.CompilerParams(
            collective_id=0, has_side_effects=True, vmem_limit_bytes=32 * 2**20
        ),
    )(*operands)
    mixed, final = pl.pallas_call(
        hand_over,
        out_shape=(
            jax.ShapeDtypeStruct((ROWS, STEPS, 128), BF16),
            jax.ShapeDtypeStruct((ROWS, HEADS * DV, DK), BF16),
        ),
        in_specs=[vmem, vmem],
        out_specs=(hbm, hbm),
        scratch_shapes=[dma((PIECES + 1,))],
        compiler_params=pltpu.CompilerParams(vmem_limit_bytes=32 * 2**20),
    )(mixed, final)
    return mixed, final.reshape(ROWS, HEADS, DV, DK)


def solution(mesh):
    return jax.shard_map(
        body,
        mesh=mesh,
        in_specs=(
            P("dp", "tensor", None, None),
            P("dp"),
            P("dp", None, "tensor"),
            P("dp", None, "tensor"),
            P("dp", None, "tensor"),
            P("dp", None, "tensor"),
            P("dp", None, None, "tensor"),
            P("tensor"),
            P("tensor"),
            P(),
            P("tensor", None),
        ),
        out_specs=(P("dp", None, "tensor"), P("dp", "tensor", None, None)),
        check_vma=False,
    )
```

```python
import functools

import jax
import jax.numpy as jnp
from jax import lax
from jax.experimental import pallas as pl
from jax.experimental.pallas import tpu as pltpu
from jax.sharding import PartitionSpec as P

MESH = pl.DeviceIdType.MESH
F32 = jnp.float32
BF16 = jnp.bfloat16
NX, NZ = 4, 8
ROWS, STEPS, DK, DV, HEADS = 32, 4, 128, 128, 2
SAMPLES = 16
TAIL = 40
HEAD = HEADS * DV - TAIL
FIRST, APART = 14, 3
LAG_T = 3
CHUNKS = 2
PIECES = 4
CROWS = ROWS * STEPS // CHUNKS
PAIRS = [(s, t) for t in range(STEPS) for s in range(t + 1)]


def split(value):
    high = value.astype(BF16).astype(F32)
    return high, value - high


def kernel(
    own, slot_in, q_in, k_in, v_in, gate_in, decay_in, rate_in, bias_in, gain_in, weight_in,
    mixed, final,
    slot, qb, kb, vb, gb, db, rate, bias, gain, weight,
    g, q32, k32, v32, g32, dt, kq, kq2, kq3, kl, ca, cb, cc, cd, ce, gs, gk, wl, hid,
    wout, wgot, wall, hout, hgot, mine, got2, got3, acc, near, m32,
    zr, xrp, xrm, xo, zsr, zsl, xsp, xsm, fsp, fsm,
    ar, asd, azr, azsr, azsl, wsem, s1, r1, s2, r2, s3, r3, lsem, isem, far_in,
):
    dp = lax.axis_index("dp")
    tn = lax.axis_index("tensor")
    x = dp // NZ
    z = dp % NZ
    xp = (x + 1) % NX
    xm = (x + 3) % NX
    y = tn // 4
    zh = (tn // 2) % 2
    core = tn % 2

    def tensor_of(yy, zz, cc_):
        return (yy * 2 + zz) * 2 + cc_

    def rc(src, dst, ss, rs, xx, zz):
        return pltpu.make_async_remote_copy(
            src_ref=src, dst_ref=dst, send_sem=ss, recv_sem=rs,
            device_id=(xx * NZ + zz, tn), device_id_type=MESH,
        )

    def tc(src, dst, ss, rs, to):
        return pltpu.make_async_remote_copy(
            src_ref=src, dst_ref=dst, send_sem=ss, recv_sem=rs,
            device_id=(dp, to), device_id_type=MESH,
        )

    local = pltpu.make_async_copy(own, g.at[x, z], lsem)
    inputs = [
        pltpu.make_async_copy(src, dst, isem.at[i])
        for i, (src, dst) in enumerate(
            (
                (k_in, kb), (q_in, qb), (v_in, vb), (gate_in, gb), (decay_in, db), (rate_in, rate),
                (bias_in, bias), (gain_in, gain), (slot_in, slot), (weight_in, weight),
            )
        )
    ]

    bar = pltpu.get_barrier_semaphore()

    def sig(d, t):
        pl.semaphore_signal(bar, inc=1, device_id=(d, t), device_id_type=MESH)

    partner = tensor_of(y, zh, 1 - core)
    far = tensor_of(y, 1 - zh, core)

    @pl.when(zh == 0)
    def _():
        sig(dp, far)

    sig(dp, tensor_of((y + 2) % 4, zh, core))
    sig(dp, tensor_of((y + 1) % 4, zh, core))
    sig(dp, tensor_of((y + 3) % 4, zh, core))
    sig(xp * NZ + z, tn)
    sig(xm * NZ + z, tn)

    @pl.when(z > 0)
    def _():
        sig(dp - 1, tn)

    @pl.when(z < NZ - 1)
    def _():
        sig(dp + 1, tn)

    sig(dp, partner)
    edge = jnp.logical_or(z == 0, z == NZ - 1)

    @pl.when(jnp.logical_and(edge, zh == 0))
    def _():
        pl.semaphore_wait(bar, 7)

    @pl.when(jnp.logical_xor(edge, zh == 0))
    def _():
        pl.semaphore_wait(bar, 8)

    @pl.when(jnp.logical_and(jnp.logical_not(edge), zh == 1))
    def _():
        pl.semaphore_wait(bar, 9)

    @pl.when(zh == 1)
    def _():
        pl.semaphore_signal(far_in, inc=1, device_id=(dp, far), device_id_type=MESH)

    def blk(xx, zp, h):
        return g.at[xx, zp, h, pl.ds(0, HEAD)]

    def z_right(zp, h, src):
        return rc(src, blk(x, zp, h), zsr.at[zp, h], zr.at[zp, h], x, z + 1)

    def z_left(zp, h, src):
        return rc(src, blk(x, zp, h), zsl.at[zp, h], zr.at[zp, h], x, z - 1)

    def x_plus(zp, h, src):
        return rc(src, blk(x, zp, h), xsp.at[zp, h], xrp.at[zp, h], xp, z)

    def x_minus(zp, h, src):
        return rc(src, blk(x, zp, h), xsm.at[zp, h], xrm.at[zp, h], xm, z)

    def f_plus(zp):
        return rc(blk(xm, zp, 0), blk(xm, zp, 0), fsp.at[zp], xo.at[zp, 0], xp, z)

    def f_minus(zp):
        return rc(blk(xp, zp, 1), blk(xp, zp, 1), fsm.at[zp], xo.at[zp, 1], xm, z)

    def tail(xx):
        return g.at[xx, z, :, pl.ds(HEAD, TAIL)]

    def tail_half(xx, h):
        return g.at[xx, z, h, pl.ds(HEAD, TAIL)]

    def t_plus(src):
        return rc(src, tail(x), asd.at[0], ar.at[0], xp, z)

    def t_minus(src):
        return rc(src, tail(x), asd.at[1], ar.at[1], xm, z)

    def tf_plus():
        return rc(tail_half(xm, 0), tail_half(xm, 0), asd.at[2], ar.at[2], xp, z)

    def tf_minus():
        return rc(tail_half(xp, 1), tail_half(xp, 1), asd.at[3], ar.at[3], xm, z)

    def tails(zp):
        return g.at[:, zp, :, pl.ds(HEAD, TAIL)]

    def tz_right(zp):
        return rc(tails(zp), tails(zp), azsr.at[zp], azr.at[zp], x, z + 1)

    def tz_left(zp):
        return rc(tails(zp), tails(zp), azsl.at[zp], azr.at[zp], x, z - 1)

    t_plus(own.at[:, pl.ds(HEAD, TAIL)]).start()
    t_minus(own.at[:, pl.ds(HEAD, TAIL)]).start()
    for h in range(2):
        src = own.at[h, pl.ds(0, HEAD)]

        @pl.when(z < NZ - 1)
        def _():
            z_right(z, h, src).start()

        @pl.when(z > 0)
        def _():
            z_left(z, h, src).start()

        x_plus(z, h, src).start()
        x_minus(z, h, src).start()
    local.start()
    for copy in inputs:
        copy.start()
    rc(tail(xm), tail(xm), asd.at[0], ar.at[0], xp, z).wait_recv()
    tf_plus().start()
    rc(tail(xp), tail(xp), asd.at[1], ar.at[1], xm, z).wait_recv()
    tf_minus().start()

    def keys_in(i, part, value):
        kq3[part, pl.ds(i, ROWS, stride=16), :] = value

    def prepare_keys():
        for copy in inputs:
            copy.wait()
        for src, dst in ((kb, k32), (qb, q32), (vb, v32), (gb, g32)):
            dst[...] = src[...].astype(F32)
        for n in range(STEPS * 2):
            dt[pl.ds(2 * n, 2), pl.ds(0, ROWS)] = db[n // 2, n % 2]
        for i in range(2 * STEPS):
            raw = k32[:, i, :] if i < STEPS else q32[:, i - STEPS, :]
            one = raw * lax.rsqrt(jnp.sum(raw * raw, axis=1, keepdims=True) + 1e-6)
            if i >= STEPS:
                one = one * (DK**-0.5)
            kq[i] = one
            high, low = split(one)
            keys_in(i, 0, high)
            keys_in(i, 1, high)
            keys_in(i + 8, 0, low)
            keys_in(i + 8, 1, jnp.zeros_like(low))
            if i < STEPS:
                kl[pl.ds(i, ROWS, stride=16), :] = high
                kl[pl.ds(i + 4, ROWS, stride=16), :] = high
                kl[pl.ds(i + 8, ROWS, stride=16), :] = low
                kl[pl.ds(i + 12, ROWS, stride=16), :] = jnp.zeros_like(low)

        for part in range(2):
            kq2[:, pl.ds(part * DK, DK)] = kq3[part]

    def prepare_gates():
        shape = (ROWS, DV)
        scalars = jnp.transpose(dt[...])
        keys = [kq[i] for i in range(2 * STEPS)]
        kk, kqd = {}, {}
        for s, t in PAIRS:
            if s < t:
                kk[s, t] = jnp.sum(keys[s] * keys[t], axis=1, keepdims=True)
            kqd[s, t] = jnp.sum(keys[s] * keys[STEPS + t], axis=1, keepdims=True)
        for h in range(HEADS):
            alpha = []
            for t in range(STEPS):
                d = scalars[0:ROWS, t * 4 + h : t * 4 + h + 1] + bias[h]
                soft = jnp.maximum(d, 0.0) + jnp.log1p(jnp.exp(-jnp.abs(d)))
                alpha.append(jnp.exp(-rate[h] * soft))
                b = scalars[0:ROWS, t * 4 + 2 + h : t * 4 + 3 + h]
                cb[h, t] = jnp.broadcast_to(1.0 / (1.0 + jnp.exp(-b)), shape)
            for t in range(STEPS):
                run = None
                for s in range(t, -1, -1):
                    n = PAIRS.index((s, t))
                    dot = kqd[s, t]
                    cd[h, n] = jnp.broadcast_to(dot if run is None else run * dot, shape)
                    if s < t:
                        cc[h, n] = jnp.broadcast_to(run * kk[s, t], shape)
                    if t == STEPS - 1:
                        ce[h, s] = jnp.broadcast_to(
                            jnp.ones_like(dot) if run is None else run, shape
                        )
                    run = alpha[s] if run is None else run * alpha[s]
                ca[h, t] = jnp.broadcast_to(run, shape)
                gate = g32[:, t, pl.ds(h * DV, DV)]
                gs[h, t] = gain[...] * gate / (1.0 + jnp.exp(-gate))

    def columns(b, cr):
        return pl.ds(pl.multiple_of((2 * b + cr) * 128, 128), 128)

    def weights_over():
        return tc(wout, wgot, wsem.at[0], wsem.at[1], partner)

    def hidden_over(h):
        return tc(hout.at[h], hgot.at[h], s1.at[h], r1.at[h], partner)

    def forward(zp):
        rc(blk(xm, zp, 0), blk(xm, zp, 0), fsp.at[zp], xrp.at[zp, 0], xp, z).wait_recv()
        f_plus(zp).start()
        rc(blk(xp, zp, 1), blk(xp, zp, 1), fsm.at[zp], xrm.at[zp, 1], xm, z).wait_recv()
        f_minus(zp).start()

    def gather_step(s, carry):
        zl = z - s
        zg = z + s
        for h in range(2):

            @pl.when(jnp.logical_and(s < NZ, zl >= 0))
            def _():
                z_right(zl, h, blk(x, zl, h)).wait_recv()

                @pl.when(z < NZ - 1)
                def _():
                    z_right(zl, h, blk(x, zl, h)).start()

                x_plus(zl, h, blk(x, zl, h)).start()
                x_minus(zl, h, blk(x, zl, h)).start()

            @pl.when(jnp.logical_and(s < NZ, zg < NZ))
            def _():
                z_left(zg, h, blk(x, zg, h)).wait_recv()

                @pl.when(z > 0)
                def _():
                    z_left(zg, h, blk(x, zg, h)).start()

                x_plus(zg, h, blk(x, zg, h)).start()
                x_minus(zg, h, blk(x, zg, h)).start()

        d = s - LAG_T

        @pl.when(d == 0)
        def _():
            rc(tail_half(x, 0), tail_half(x, 0), asd.at[2], ar.at[2], xp, z).wait_recv()
            rc(tail_half(x, 1), tail_half(x, 1), asd.at[3], ar.at[3], xm, z).wait_recv()
            local.wait()

            @pl.when(z < NZ - 1)
            def _():
                tz_right(z).start()

            @pl.when(z > 0)
            def _():
                tz_left(z).start()

        @pl.when(jnp.logical_and(d >= 1, z - d >= 0))
        def _():
            tz_right(z - d).wait_recv()

            @pl.when(z < NZ - 1)
            def _():
                tz_right(z - d).start()

        @pl.when(jnp.logical_and(d >= 1, z + d < NZ))
        def _():
            tz_left(z + d).wait_recv()

            @pl.when(z > 0)
            def _():
                tz_left(z + d).start()

        def onward(r, carry):
            both = jnp.minimum(z, NZ - 1 - z)
            paired = r <= 2 * both
            away = jnp.where(paired, (r + 1) // 2, r - both)
            below = jnp.where(paired, r % 2 == 1, z >= NZ // 2)
            forward(jnp.where(below, z - away, z + away))
            return carry

        def rank_at(quarter):
            return jnp.clip((quarter - FIRST + APART - 1 + 16 * APART) // APART - 16, 0, NZ)

        lax.fori_loop(rank_at(4 * s), rank_at(4 * s + 4), onward, 0)

        @pl.when(s == 3)
        def _():
            for b in range(8):
                wout[b] = weight[:, columns(b, 1 - core)].astype(F32)
                wall[b, pl.ds(0, HEADS * DV)] = weight[:, columns(b, core)]
            weights_over().start()

        @pl.when(s == 6)
        def _():
            weights_over().wait()
            for b in range(8):
                wall[b, pl.ds(HEADS * DV, HEADS * DV)] = wgot[b].astype(BF16)

        @pl.when(s == 1)
        def _():
            prepare_keys()

        @pl.when(s == 2)
        def _():
            prepare_gates()

        return carry

    lax.fori_loop(1, max(NZ + LAG_T, (FIRST + (NZ - 1) * APART) // 4 + 1), gather_step, 0)

    def last_blocks(zp, carry):
        rc(blk(xm, zp, 1), blk(xm, zp, 1), xsp.at[zp, 1], xrp.at[zp, 1], xp, z).wait_recv()
        rc(blk(xp, zp, 0), blk(xp, zp, 0), xsm.at[zp, 0], xrm.at[zp, 0], xm, z).wait_recv()
        f_plus(zp).wait_recv()
        f_minus(zp).wait_recv()
        return carry

    lax.fori_loop(0, NZ, last_blocks, 0)

    contract = (((1,), (1,)), ((), ()))

    def state_of(r):
        p = slot[r] // SAMPLES
        return g[p // (2 * NZ), (p // 2) % NZ, p % 2]

    def recall(r, carry):
        high, low = split(state_of(r))
        halves = jnp.concatenate([high.astype(BF16), low.astype(BF16)], axis=1)
        both = kq2[pl.ds(pl.multiple_of(r * 16, 16), 16), :].astype(BF16)
        a = lax.dot_general(both, halves, contract, preferred_element_type=F32)
        total = a[0:8] + a[8:16]
        at = pl.ds(pl.multiple_of(r * 8, 8), 8)
        gk[0, at, :] = total[:, 0:DV]
        gk[1, at, :] = total[:, DV:]
        return carry

    lax.fori_loop(0, ROWS, recall, 0, unroll=16)

    def run_steps(h, carry):
        lanes = pl.ds(pl.multiple_of(h * DV, DV), DV)
        u = []
        for t in range(STEPS):
            seen = ca[h, t] * gk[h, pl.ds(t, ROWS, stride=8), :]
            out = ca[h, t] * gk[h, pl.ds(STEPS + t, ROWS, stride=8), :]
            for s in range(t):
                seen = seen + cc[h, PAIRS.index((s, t))] * u[s]
            value = v32[:, t, lanes]
            u.append(cb[h, t] * (value - seen))
            for s in range(t + 1):
                out = out + cd[h, PAIRS.index((s, t))] * u[s]
            scale = lax.rsqrt(jnp.mean(out * out, axis=1, keepdims=True) + 1e-6)
            some = pl.ds(t * ROWS, ROWS)
            hidden = (out * scale * gs[h, t]).astype(BF16)
            hid[some, lanes] = hidden
            hout[h, some] = hidden.astype(F32)
        hidden_over(h).start()
        for s in range(STEPS):
            high, low = split(ce[h, s] * u[s])
            wl[h, pl.ds(s, ROWS, stride=16), :] = high
            wl[h, pl.ds(s + 4, ROWS, stride=16), :] = low
            wl[h, pl.ds(s + 8, ROWS, stride=16), :] = high
            wl[h, pl.ds(s + 12, ROWS, stride=16), :] = jnp.zeros_like(high)
        return carry

    lax.fori_loop(0, HEADS, run_steps, 0)

    def along_y(side, c, hop):
        at = (side, c, hop - 1)
        return tc(
            mine.at[side, c, (y + hop) % 4], got2.at[at], s2.at[at], r2.at[at],
            tensor_of((y + hop) % 4, zh, core),
        )

    def along_z(c):
        return tc(acc.at[c], got3.at[c], s3.at[c], r3.at[c], far)

    for h in range(HEADS):
        hidden_over(h).wait_recv()
        hid[:, pl.ds((HEADS + h) * DV, DV)] = hgot[h].astype(BF16)

    def product(n, carry):
        side = n // 4
        hop = (n + 2) % 4
        yy = (y + hop) % 4
        zz = (zh + 1 + side) % 2
        term = jnp.dot(hid[...], wall[yy * 2 + zz], preferred_element_type=F32)
        for c in range(CHUNKS):
            mine[side, c, yy] = term[c * CROWS : (c + 1) * CROWS]

            @pl.when(hop > 0)
            def _():
                along_y(side, c, hop).start()

        return carry

    def finish(r, carry):
        state = state_of(r)
        at = pl.ds(pl.multiple_of(r * 16, 16), 16)
        keys = kl[at, :].astype(BF16)
        for h in range(HEADS):
            update = lax.dot_general(
                wl[h, at, :].astype(BF16), keys, (((0,), (0,)), ((), ())),
                preferred_element_type=F32,
            )
            decay = ca[h, STEPS - 1, pl.ds(r, 1), :]
            final[r, pl.ds(h * DV, DV), :] = (
                decay * state[h * DV : (h + 1) * DV] + update
            ).astype(BF16)
        return carry

    lax.fori_loop(0, 4, product, 0)
    early = jnp.where(z < 4, 12, 12)
    lax.fori_loop(0, early, finish, 0)

    def summed(side, c):
        for hop in (1, 2, 3):
            along_y(side, c, hop).wait_recv()
        return mine[side, c, y] + got2[side, c, 0] + got2[side, c, 1] + got2[side, c, 2]

    @pl.when(zh == 0)
    def _():
        pl.semaphore_wait(far_in, 1)

    def send_z(c, carry):
        acc[c] = summed(0, c)
        along_z(c).start()
        return carry

    lax.fori_loop(0, CHUNKS, send_z, 0)

    lax.fori_loop(4, 8, product, 0)
    lax.fori_loop(early, ROWS, finish, 0)

    t_plus(tail(x)).wait_send()
    t_minus(tail(x)).wait_send()
    tf_plus().wait_send()
    tf_minus().wait_send()

    def sent(zp, carry):
        for h in range(2):
            x_plus(zp, h, blk(x, zp, h)).wait_send()
            x_minus(zp, h, blk(x, zp, h)).wait_send()

            @pl.when(jnp.logical_and(z < NZ - 1, zp <= z))
            def _():
                z_right(zp, h, blk(x, zp, h)).wait_send()

            @pl.when(jnp.logical_and(z > 0, zp >= z))
            def _():
                z_left(zp, h, blk(x, zp, h)).wait_send()

        @pl.when(jnp.logical_and(z < NZ - 1, zp <= z))
        def _():
            tz_right(zp).wait_send()

        @pl.when(jnp.logical_and(z > 0, zp >= z))
        def _():
            tz_left(zp).wait_send()

        f_plus(zp).wait_send()
        f_minus(zp).wait_send()
        return carry

    lax.fori_loop(0, NZ, sent, 0)

    def left(n, carry):
        for hop in (1, 2, 3):
            along_y(n // CHUNKS, n % CHUNKS, hop).wait_send()
        return carry

    lax.fori_loop(0, 2 * CHUNKS, left, 0)
    for h in range(HEADS):
        hidden_over(h).wait_send()

    def keep(c, carry):
        near[c] = summed(1, c)
        return carry

    lax.fori_loop(0, CHUNKS, keep, 0)

    def gather_z(c, carry):
        along_z(c).wait_recv()
        for i in range(STEPS // CHUNKS):
            some = pl.ds(i * ROWS, ROWS)
            m32[:, c * (STEPS // CHUNKS) + i, :] = near[c, some] + got3[c, some]
        return carry

    lax.fori_loop(0, CHUNKS, gather_z, 0)
    mixed[...] = m32[...].astype(BF16)

    for c in range(CHUNKS):
        along_z(c).wait_send()


def hand_over(mixed_in, final_in, mixed, final, sem):
    size = ROWS // PIECES
    copies = [
        pltpu.make_async_copy(final_in.at[pl.ds(i * size, size)], final.at[pl.ds(i * size, size)], sem.at[i])
        for i in range(PIECES)
    ]
    copies.append(pltpu.make_async_copy(mixed_in, mixed, sem.at[PIECES]))
    for copy in copies:
        copy.start()
    for copy in copies:
        copy.wait()


def body(
    owner_states, sample_slot, query_in, key_in, value_in, gate_in, decay_in,
    decay_rate, dt_bias, norm_gain, out_weight,
):
    vmem = pl.BlockSpec(memory_space=pltpu.VMEM)
    hbm = pl.BlockSpec(memory_space=pltpu.HBM)
    dma = pltpu.SemaphoreType.DMA
    npair = len(PAIRS)
    operands = [
        pltpu.with_memory_space_constraint(value, pltpu.HBM)
        for value in (
            owner_states.reshape(2, HEADS * DV, DK),
            sample_slot,
            query_in,
            key_in,
            value_in,
            gate_in,
            decay_in.transpose(1, 2, 3, 0),
            decay_rate,
            dt_bias,
            norm_gain.reshape(1, DV),
            out_weight,
        )
    ]
    mixed, final = pl.pallas_call(
        kernel,
        out_shape=(
            pltpu.VMEM((ROWS, STEPS, 128), BF16),
            pltpu.VMEM((ROWS, HEADS * DV, DK), BF16),
        ),
        in_specs=[hbm] * 11,
        out_specs=(vmem, vmem),
        scratch_shapes=[
            pltpu.SMEM((ROWS,), jnp.int32),
            pltpu.VMEM((ROWS, STEPS, DK), BF16),
            pltpu.VMEM((ROWS, STEPS, DK), BF16),
            pltpu.VMEM((ROWS, STEPS, HEADS * DV), BF16),
            pltpu.VMEM((ROWS, STEPS, HEADS * DV), BF16),
            pltpu.VMEM((STEPS, 2, HEADS, ROWS), F32),
            pltpu.SMEM((HEADS,), F32),
            pltpu.SMEM((HEADS,), F32),
            pltpu.VMEM((1, DV), F32),
            pltpu.VMEM((HEADS * DV, 2048), BF16),
            pltpu.VMEM((NX, NZ, 2, HEADS * DV, DK), F32),
            pltpu.VMEM((ROWS, STEPS, DK), F32),
            pltpu.VMEM((ROWS, STEPS, DK), F32),
            pltpu.VMEM((ROWS, STEPS, HEADS * DV), F32),
            pltpu.VMEM((ROWS, STEPS, HEADS * DV), F32),
            pltpu.VMEM((STEPS * 2 * HEADS, 128), F32),
            pltpu.VMEM((2 * STEPS, ROWS, DK), F32),
            pltpu.VMEM((ROWS * 16, 2 * DK), F32),
            pltpu.VMEM((2, ROWS * 16, DK), F32),
            pltpu.VMEM((ROWS * 16, DK), F32),
            pltpu.VMEM((HEADS, STEPS, ROWS, DV), F32),
            pltpu.VMEM((HEADS, STEPS, ROWS, DV), F32),
            pltpu.VMEM((HEADS, npair, ROWS, DV), F32),
            pltpu.VMEM((HEADS, npair, ROWS, DV), F32),
            pltpu.VMEM((HEADS, STEPS, ROWS, DV), F32),
            pltpu.VMEM((HEADS, STEPS, ROWS, DV), F32),
            pltpu.VMEM((HEADS, ROWS * 8, DV), F32),
            pltpu.VMEM((HEADS, ROWS * 16, DV), F32),
            pltpu.VMEM((ROWS * STEPS, 2 * HEADS * DV), BF16),
            pltpu.VMEM((8, HEADS * DV, 128), F32),
            pltpu.VMEM((8, HEADS * DV, 128), F32),
            pltpu.VMEM((8, 2 * HEADS * DV, 128), BF16),
            pltpu.VMEM((HEADS, ROWS * STEPS, DV), F32),
            pltpu.VMEM((HEADS, ROWS * STEPS, DV), F32),
            pltpu.VMEM((2, CHUNKS, 4, CROWS, 128), F32),
            pltpu.VMEM((2, CHUNKS, 3, CROWS, 128), F32),
            pltpu.VMEM((CHUNKS, CROWS, 128), F32),
            pltpu.VMEM((CHUNKS, CROWS, 128), F32),
            pltpu.VMEM((CHUNKS, CROWS, 128), F32),
            pltpu.VMEM((ROWS, STEPS, 128), F32),
        ]
        + [dma((NZ, 2)) for _ in range(8)]
        + [dma((NZ,)), dma((NZ,)), dma((4,)), dma((4,)), dma((NZ,)), dma((NZ,)), dma((NZ,))]
        + [dma((2,)), dma((HEADS,)), dma((HEADS,)), dma((2, CHUNKS, 3)), dma((2, CHUNKS, 3))]
        + [dma((CHUNKS,)), dma((CHUNKS,)), dma, dma((10,)), pltpu.SemaphoreType.REGULAR],
        compiler_params=pltpu.CompilerParams(
            collective_id=0, has_side_effects=True, vmem_limit_bytes=32 * 2**20
        ),
    )(*operands)
    mixed, final = pl.pallas_call(
        hand_over,
        out_shape=(
            jax.ShapeDtypeStruct((ROWS, STEPS, 128), BF16),
            jax.ShapeDtypeStruct((ROWS, HEADS * DV, DK), BF16),
        ),
        in_specs=[vmem, vmem],
        out_specs=(hbm, hbm),
        scratch_shapes=[dma((PIECES + 1,))],
        compiler_params=pltpu.CompilerParams(vmem_limit_bytes=32 * 2**20),
    )(mixed, final)
    return mixed, final.reshape(ROWS, HEADS, DV, DK)


def solution(mesh):
    return jax.shard_map(
        body,
        mesh=mesh,
        in_specs=(
            P("dp", "tensor", None, None),
            P("dp"),
            P("dp", None, "tensor"),
            P("dp", None, "tensor"),
            P("dp", None, "tensor"),
            P("dp", None, "tensor"),
            P("dp", None, None, "tensor"),
            P("tensor"),
            P("tensor"),
            P(),
            P("tensor", None),
        ),
        out_specs=(P("dp", None, "tensor"), P("dp", "tensor", None, None)),
        check_vma=False,
    )
```
